1024 devices in a mesh: group: 16 (over z, core), local: 64 (over y, x).
Axes of the slice: x: 8, y: 8, z: 8, core: 2. Of those that a mesh axis runs over, the one named last changes fastest.
Arguments:
- tokens: bfloat16 [2048, 4096], P(('group', 'local')), may hold values from -6 to 6
- cotangent: bfloat16 [2048, 4096], P(('group', 'local')), may hold values from -6 to 6
- gates: bfloat16 [2048, 8], P(('group', 'local')), may hold values from 0.049804688 to 1
- expert_ids: int32 [2048, 8], P(('group', 'local')), may hold values from 0 to 127, as said below
- capacity: int32 [128], replicated, may hold values from 5 to 10, as said below
- w_gate: bfloat16 [524288, 1024], P(('group', 'local')), may hold values from -0.09375 to 0.09375
- w_up: bfloat16 [524288, 1024], P(('group', 'local')), may hold values from -0.09375 to 0.09375
- w_down: bfloat16 [1024, 524288], P(None, ('group', 'local')), may hold values from -0.1875 to 0.1875
Outputs:
- mixed: bfloat16 [2048, 4096], P(('group', 'local'))
- token_grad: bfloat16 [2048, 4096], P(('group', 'local'))
The draws below stay inside these ranges and needn't reach their ends.
Inputs may be any that keep to these rules, and one draw needn't show every extreme that they name: `expert_ids`: each row names 8 different experts, all of them in at most 4 groups, expert e lying in group e // 8. capacity[e] is the most rows that expert e takes from the tokens of one group.
All inputs are finite; a program needn't handle non-finite values.
Results may differ from the reference program's by a relative error of at most 0.007.
Values may be sent and summed in bfloat16 or wider, within the bound.
A program may use at most 32 MiB of HBM per device.

```python
import math
import jax
import jax.numpy as jnp
from jax import lax

D = 4096
FF = 1024
TOK_DEV = 2
GROUPS = 16
NODES = 4
EXP_GROUP = 8
EXPERTS = 128
TOPK = 8
GTOK = 128
CAPG = 10
ROWS = 160
TOKENS = 2048


def favoured_expert(key):
    return jax.random.randint(key, (), 0, EXPERTS)


def draw_expert_ids(key, part):
    favoured = favoured_expert(key)
    key = jax.random.fold_in(key, 11)
    key_perm, key_score, key_pop = jax.random.split(key, 3)
    block_count = TOKENS // TOK_DEV
    perms = jax.vmap(lambda one_key: jax.random.permutation(one_key, GROUPS))(jax.random.split(key_perm, block_count))
    positions = (jnp.arange(TOK_DEV)[:, None] * NODES + jnp.arange(NODES)[None, :]) % GROUPS
    chosen_groups = perms[:, positions].reshape(TOKENS, NODES)
    cand_width = NODES * EXP_GROUP
    candidates = (chosen_groups[:, :, None] * EXP_GROUP + jnp.arange(EXP_GROUP)[None, None, :]).reshape(TOKENS, cand_width)
    popular = jax.random.randint(key_pop, (EXPERTS,), 0, 12)
    popular = jnp.where(jnp.arange(EXPERTS) == favoured, 1000, popular)
    noise = jax.random.randint(key_score, (TOKENS, cand_width), 0, 16)
    scores = (noise + popular[candidates]) * cand_width + jnp.arange(cand_width)[None, :]
    top_scores, picks = lax.top_k(scores, TOPK)
    return jnp.take_along_axis(candidates, picks, axis=1).astype(jnp.int32)


def draw_capacity(key, part):
    favoured = favoured_expert(key)
    key = jax.random.fold_in(key, 23)
    limits = jax.random.randint(key, (EXPERTS,), CAPG // 2, CAPG + 1)
    return jnp.where(jnp.arange(EXPERTS) == favoured, CAPG, limits).astype(jnp.int32)


def levels(key, extent, cuts, low, high):
    def one(axis_at, parts):
        heights = jax.random.uniform(jax.random.fold_in(jax.random.fold_in(key, 6), axis_at), (parts,), jnp.float32, low / len(cuts), high / len(cuts))
        return jnp.repeat(jnp.exp(heights), extent[axis_at] // parts).reshape((-1,) + (1,) * (len(extent) - axis_at - 1))

    loudness = one(*cuts[0])
    for cut in cuts[1:]:
        loudness = loudness * one(*cut)
    return loudness


def normal_values(rng, dims, width, reach, cuts=(), kind=jnp.bfloat16):
    drawn = width * jax.random.normal(rng, dims, jnp.float32)
    if cuts:
        drawn = drawn * levels(rng, dims, cuts, -0.22, 0.18)
    return jnp.clip(drawn, -reach, reach).astype(kind)


def setup_inputs(seed: int = 0) -> dict:
    splits = jax.random.split(jax.random.key(seed), 9)
    tokens = normal_values(splits[0], (TOKENS, D), 1.0, 6.0, ((0, 1024),))
    cotangent = normal_values(splits[1], (TOKENS, D), 1.0, 6.0, ((0, 1024),))
    gates = jnp.clip(jnp.exp(math.log(1.0) - 2.9996462 * jax.random.uniform(splits[2], (TOKENS, TOPK), jnp.float32) ** levels(splits[2], (TOKENS, TOPK), ((0, 1024),), -0.2, 0.2)), 0.049804688, 1.0).astype(jnp.bfloat16)
    expert_ids = draw_expert_ids(jax.random.fold_in(splits[8], 71), 0)
    capacity = draw_capacity(jax.random.fold_in(splits[8], 71), 0)
    w_gate = normal_values(splits[5], (EXPERTS * D, FF), D ** -0.5, 0.09375, ((0, 1024),))
    w_up = normal_values(splits[6], (EXPERTS * D, FF), D ** -0.5, 0.09375, ((0, 1024),))
    w_down = normal_values(splits[7], (FF, EXPERTS * D), FF ** -0.5, 0.1875, ((1, 1024),))
    return {"tokens": tokens, "cotangent": cotangent, "gates": gates, "expert_ids": expert_ids, "capacity": capacity, "w_gate": w_gate, "w_up": w_up, "w_down": w_down}


def expert_pass(rows_in, rows_back, weight_gate, weight_up, weight_down):
    gate_pre = jnp.dot(rows_in, weight_gate, preferred_element_type=jnp.float32)
    up_pre = jnp.dot(rows_in, weight_up, preferred_element_type=jnp.float32)
    sigmoid_gate = jax.nn.sigmoid(gate_pre)
    activated = gate_pre * sigmoid_gate
    hidden = (activated * up_pre).astype(jnp.bfloat16)
    output = jnp.dot(hidden, weight_down, preferred_element_type=jnp.float32).astype(jnp.bfloat16)
    d_hidden = jnp.dot(rows_back, weight_down.T, preferred_element_type=jnp.float32)
    d_gate = (d_hidden * up_pre * sigmoid_gate * (1.0 + gate_pre * (1.0 - sigmoid_gate))).astype(jnp.bfloat16)
    d_up = (d_hidden * activated).astype(jnp.bfloat16)
    grad_in = jnp.dot(d_gate, weight_gate.T, preferred_element_type=jnp.float32)
    grad_in = grad_in + jnp.dot(d_up, weight_up.T, preferred_element_type=jnp.float32)
    return output, grad_in.astype(jnp.bfloat16)


def reference(tokens, cotangent, gates, expert_ids, capacity, w_gate, w_up, w_down):
    inputs_all = tokens.astype(jnp.float32).reshape(GROUPS, GTOK, D)
    backs_all = cotangent.astype(jnp.float32).reshape(GROUPS, GTOK, D)
    chosen_ids = expert_ids.reshape(GROUPS, GTOK, TOPK)
    gate_values = gates.astype(jnp.float32).reshape(GROUPS, GTOK, TOPK)
    gate_all = w_gate.reshape(EXPERTS, D, FF)
    up_all = w_up.reshape(EXPERTS, D, FF)
    down_all = w_down.reshape(FF, EXPERTS, D)
    slot_ids = jnp.arange(CAPG, dtype=jnp.int32)

    def visit(carry, expert):
        out_sum, grad_sum = carry
        matches = chosen_ids == expert
        chosen = jnp.any(matches, axis=-1).astype(jnp.int32)
        weight = jnp.sum(jnp.where(matches, gate_values, jnp.float32(0.0)), axis=-1)
        rank_pair = jnp.cumsum(chosen, axis=1) - chosen
        kept = (chosen > 0) & (rank_pair < capacity[expert])
        select = (kept[:, None, :] & (rank_pair[:, None, :] == slot_ids[None, :, None])).astype(jnp.float32)
        rows_in = jnp.einsum("qct,qtd->qcd", select, inputs_all, precision=lax.Precision.HIGHEST)
        rows_back = jnp.einsum("qct,qtd->qcd", select, backs_all, precision=lax.Precision.HIGHEST)
        output, grad_in = expert_pass(rows_in.astype(jnp.bfloat16).reshape(ROWS, D),
                                      rows_back.astype(jnp.bfloat16).reshape(ROWS, D),
                                      gate_all[expert], up_all[expert], down_all[:, expert, :])
        weighted = select * weight[:, None, :]
        out_sum = out_sum + jnp.einsum("qct,qcd->qtd", weighted, output.astype(jnp.float32).reshape(GROUPS, CAPG, D), precision=lax.Precision.HIGHEST)
        grad_sum = grad_sum + jnp.einsum("qct,qcd->qtd", weighted, grad_in.astype(jnp.float32).reshape(GROUPS, CAPG, D), precision=lax.Precision.HIGHEST)
        return (out_sum, grad_sum), None

    start = (jnp.zeros((GROUPS, GTOK, D), jnp.float32), jnp.zeros((GROUPS, GTOK, D), jnp.float32))
    (out_sum, grad_sum), unused = lax.scan(visit, start, jnp.arange(EXPERTS, dtype=jnp.int32))
    return out_sum.reshape(TOKENS, D).astype(jnp.bfloat16), grad_sum.reshape(TOKENS, D).astype(jnp.bfloat16)
```

```python
import functools

import jax
import jax.numpy as jnp
from jax import lax
from jax.experimental import pallas as pl
from jax.experimental.pallas import tpu as pltpu
from jax.sharding import PartitionSpec as P

LANES = 128
BF16 = jnp.bfloat16
F32 = jnp.float32
MESH = pl.DeviceIdType.MESH
CONTRACT_LAST = (((1,), (1,)), ((), ()))


def matmul(a, b):
    return jnp.dot(a, b, preferred_element_type=F32)


def matmul_t(a, b):
    return lax.dot_general(a, b, CONTRACT_LAST, preferred_element_type=F32)


def moe_kernel(
    nx, ny, ng, slots,
    tokens, cotangent, gates, ids, cap, wg_hbm, wu_hbm, wd_hbm,
    mixed, token_grad,
    wg, wu, wd, meta2, xs_f, xs, xr, xf, yb, wsel_t, rows_f, zs, zr, acts,
    rs_out, rs_in, hid, acc, ps, pf, ys, yr, xo, xi, final,
    w_sem, x_sem, y_sem, z_sem, rs_sem, ag_sem, r_sem, ys_sem, xo_sem,
):
    tok, width = tokens.shape
    top = ids.shape[1]
    w = wg.shape[0]
    fc = wg.shape[1] // nx
    nj = w // LANES
    ns = 2 * nj
    block = nx * tok
    group = ny * block
    rows = ng * slots
    half = rows // 2
    used = slots * nj
    padded = zs.shape[3]
    hx, hy = nx // 2, ny // 2

    g = lax.axis_index("group")
    at = lax.axis_index("local")
    y = lax.div(at, nx)
    x = lax.rem(at, nx)

    def x_dev(k):
        return {"local": y * nx + lax.rem(x + k + nx, nx)}

    def y_dev(k):
        return {"local": lax.rem(y + k + ny, ny) * nx + x}

    def g_dev(k):
        return {"group": lax.rem(g + k, ng)}

    def each(low, high, body):
        def step(i, carry):
            body(i)
            return carry
        lax.fori_loop(low, high, step, 0)

    def remote(src, dst, sems, index, device):
        return pltpu.make_async_remote_copy(
            src_ref=src, dst_ref=dst, send_sem=sems.at[(0,) + index], recv_sem=sems.at[(1,) + index],
            device_id=device, device_id_type=MESH)

    weights = [pltpu.make_async_copy(a, b, w_sem.at[i])
               for i, (a, b) in enumerate(((wg_hbm, wg), (wu_hbm, wu), (wd_hbm, wd)))]
    for copy in weights:
        copy.start()

    barrier = pltpu.get_barrier_semaphore()

    def greet(device):
        pl.semaphore_signal(barrier, inc=1, device_id=device, device_id_type=MESH)

    each(1, nx, lambda k: greet(x_dev(k)))
    each(1, ny, lambda k: greet(y_dev(k)))
    each(1, ng, lambda k: greet(g_dev(k)))

    meta2[...] = jnp.zeros_like(meta2)
    meta2[:, 0:top] = ids[...].astype(F32)
    meta2[:, top:2 * top] = gates[...].astype(F32)
    xs_f[...] = jnp.zeros_like(xs_f)

    def cut(dest):
        start = pl.multiple_of(dest * w, LANES)
        for side, ref in enumerate((tokens, cotangent)):
            v = ref[:, pl.ds(start, w)].astype(F32)
            for i in range(tok):
                for j in range(nj):
                    r = i * ns + side * nj + j
                    xs_f[dest, r:r + 1, :] = v[i:i + 1, j * LANES:(j + 1) * LANES]
        for i in range(tok):
            r = tok * ns + i * ns
            xs_f[dest, r:r + 1, :] = meta2[i:i + 1, :]

    each(0, nx, cut)
    xs[...] = xs_f[...].astype(BF16)
    xr[pl.ds(x, 1)] = xs[pl.ds(x, 1)]
    pl.semaphore_wait(barrier, nx + ny + ng - 3)

    def x_copy(k, peer):
        return remote(xs.at[lax.rem(x + k, nx)], xr.at[peer], x_sem, (k,), x_dev(k))

    each(1, nx, lambda k: x_copy(k, x).start())
    each(1, nx, lambda k: x_copy(k, lax.rem(x - k + nx, nx)).wait_recv())

    tr = tok * ns
    xf[0] = xr[:, 0:tr].astype(F32).reshape(nx * tr, LANES)
    xf[1] = xr[:, tr:2 * tr].astype(F32).reshape(nx * tr, LANES)
    for s in range(ns):
        yb[y, s] = xf[0, pl.ds(s, block, stride=ns), :].astype(BF16)
    yb[y, ns] = xf[1, pl.ds(0, block, stride=ns), :].astype(BF16)

    cut_y = (ns + 1) // 2

    def y_part(chunk, direction, k):
        ref = yb.at[chunk]
        if k < hy:
            return ref
        return ref.at[pl.ds(0, cut_y)] if direction == 0 else ref.at[pl.ds(cut_y, ns + 1 - cut_y)]

    def y_copy(direction, k, receive=False):
        sign = 1 if direction == 0 else -1
        back = k if receive else k - 1
        chunk = lax.rem(y - sign * back + ny, ny)
        ref = y_part(chunk, direction, k)
        return remote(ref, ref, y_sem, (direction, k), y_dev(sign))

    for k in range(1, hy + 1):
        for direction in range(2):
            if k > 1:
                y_copy(direction, k - 1, True).wait_recv()
            y_copy(direction, k).start()
    for direction in range(2):
        y_copy(direction, hy, True).wait_recv()

    meta = yb[:, ns].astype(F32).reshape(group, LANES)
    expert = lax.broadcasted_iota(jnp.int32, (group, LANES), 1).astype(F32)
    hit = jnp.zeros((group, LANES), F32)
    weight = jnp.zeros((group, LANES), F32)
    for k in range(top):
        same = meta[:, k:k + 1] == expert
        hit = jnp.where(same, 1.0, hit)
        weight = jnp.where(same, meta[:, top + k:top + k + 1], weight)
    earlier = (lax.broadcasted_iota(jnp.int32, (group, group), 1)
               < lax.broadcasted_iota(jnp.int32, (group, group), 0))
    rank = matmul(jnp.where(earlier, 1.0, 0.0).astype(BF16), hit.astype(BF16))
    kept = (hit > 0.5) & (rank < cap[...].astype(F32))
    rank = jnp.where(kept, rank, -1.0).astype(BF16)
    weight = weight.astype(BF16)

    r_group = jnp.floor((lax.broadcasted_iota(jnp.int32, (rows, LANES), 0).astype(F32) + 0.5) * (1.0 / slots))
    r_expert = r_group * ny + y.astype(F32)
    pick = jnp.where(lax.broadcasted_iota(jnp.int32, (rows, LANES), 1).astype(F32) == r_expert, 1.0, 0.0).astype(BF16)
    r_at = lax.broadcasted_iota(jnp.int32, (rows, group), 0).astype(F32)
    r_slot = r_at - jnp.floor((r_at + 0.5) * (1.0 / slots)) * slots
    select = jnp.where(matmul_t(pick, rank) == r_slot, 1.0, 0.0).astype(BF16)
    c_at = lax.broadcasted_iota(jnp.int32, (group, rows), 1).astype(F32)
    c_slot = c_at - jnp.floor((c_at + 0.5) * (1.0 / slots)) * slots
    wsel_t[...] = jnp.where(matmul_t(rank, pick) == c_slot, matmul_t(weight, pick), 0.0).astype(BF16)

    def spread(side, way):
        def one(k):
            dest = lax.rem(g + k, ng)
            part = rows_f[side, pl.ds(pl.multiple_of(dest * used, 8), used), :]
            if padded > used:
                part = jnp.concatenate([part, jnp.zeros((padded - used, LANES), F32)], 0)
            return dest, part.astype(BF16)

        def go(k):
            dest, part = one(k)
            zs[way, side, dest] = part
            z_copy(way, side, k, g).start()

        dest, part = one(0)
        zr[way, side, dest] = part
        each(1, ng, go)

    def z_copy(way, side, k, peer):
        return remote(zs.at[way, side, lax.rem(g + k, ng)], zr.at[way, side, peer],
                      z_sem, (way, side, k), g_dev(k))

    def collect(way, side):
        each(1, ng, lambda k: z_copy(way, side, k, lax.rem(g - k + ng, ng)).wait_recv())
        got = zr[way, side].astype(F32)
        rows_f[2 + side] = got[:, 0:used].reshape(ng * used, LANES)
        return [rows_f[2 + side, pl.ds(j, rows, stride=nj), :].astype(BF16) for j in range(nj)]

    for side in range(2):
        for j in range(nj):
            held = yb[:, side * nj + j].reshape(group, LANES)
            rows_f[side, pl.ds(j, rows, stride=nj), :] = matmul(select, held)
        spread(side, 0)

    def lanes_of(chunk):
        return pl.ds(pl.multiple_of(chunk * fc, LANES), fc)

    def products(kind, chunk):
        here = lanes_of(chunk)
        if kind == 0:
            both = matmul(acts[0], jnp.concatenate([wg[:, here], wu[:, here]], 1))
            return [(0, both[:, 0:fc]), (1, both[:, fc:2 * fc])]
        return [(2, matmul_t(acts[1], wd[here, :]))]

    def span(direction, far):
        return pl.ds(0, rows) if not far else pl.ds(0, half) if direction == 0 else pl.ds(half, rows - half)

    def rs_copy(direction, d, m):
        part = span(direction, d == hx)
        return remote(rs_out.at[direction, d - 1, m, part], rs_in.at[direction, d - 1, m, part],
                      rs_sem, (direction, d - 1, m), x_dev(1 if direction == 0 else -1))

    def rs_step(kind, d):
        shared = products(kind, lax.rem(x + hx, nx)) if d == hx else None
        for direction in range(2):
            sign = 1 if direction == 0 else -1
            mine = shared if d == hx else products(kind, lax.rem(x + sign * d + nx, nx))
            for m, part in mine:
                if d == hx:
                    p = span(direction, True)
                    rs_out[direction, d - 1, m, p] = part[0:half].astype(BF16) if direction == 0 else part[half:rows].astype(BF16)
                else:
                    rs_copy(direction, d + 1, m).wait_recv()
                    if d + 1 == hx:
                        add = rs_in[direction, d, m, span(direction, True)].astype(F32)
                        if direction == 0:
                            part = jnp.concatenate([part[0:half] + add, part[half:rows]], 0)
                        else:
                            part = jnp.concatenate([part[0:half], part[half:rows] + add], 0)
                    else:
                        part = part + rs_in[direction, d, m].astype(F32)
                    rs_out[direction, d - 1, m] = part.astype(BF16)
                rs_copy(direction, d, m).start()

    def rs_last(kind):
        totals = []
        for m, part in products(kind, x):
            for direction in range(2):
                rs_copy(direction, 1, m).wait_recv()
                part = part + rs_in[direction, 0, m].astype(F32)
            totals.append(part)
        return totals

    def ag_copy(direction, k, m, receive=False):
        sign = 1 if direction == 0 else -1
        back = k if receive else k - 1
        chunk = lax.rem(x - sign * back + nx, nx)
        ref = hid.at[chunk, m, span(direction, k == hx)]
        return remote(ref, ref, ag_sem, (direction, k - 1, m), x_dev(sign))

    def ag_step(m, k):
        for direction in range(2):
            if k > 1:
                ag_copy(direction, k - 1, m, True).wait_recv()
            ag_copy(direction, k, m).start()

    def add_out(chunk):
        acc[0] += matmul(hid[chunk, 0], wd[lanes_of(chunk), :])

    def add_grad(chunk):
        here = lanes_of(chunk)
        acc[1] += matmul_t(jnp.concatenate([hid[chunk, 1], hid[chunk, 2]], 1),
                           jnp.concatenate([wg[:, here], wu[:, here]], 1))

    for j, part in enumerate(collect(0, 0)):
        acts[0, :, j * LANES:(j + 1) * LANES] = part
    for copy in weights:
        copy.wait()
    rs_step(0, hx)
    for j, part in enumerate(collect(0, 1)):
        acts[1, :, j * LANES:(j + 1) * LANES] = part
    for d in range(hx - 1, 0, -1):
        rs_step(0, d)
        rs_step(1, d + 1)
    gate_pre, up_pre = rs_last(0)
    sig = jax.nn.sigmoid(gate_pre)
    silu = gate_pre * sig
    hid[x, 0] = (silu * up_pre).astype(BF16)
    ag_step(0, 1)
    d_gate_by = up_pre * sig * (1.0 + gate_pre * (1.0 - sig))
    rs_step(1, 1)
    acc[...] = jnp.zeros_like(acc)
    add_out(x)
    (d_hidden,) = rs_last(1)
    hid[x, 1] = (d_hidden * d_gate_by).astype(BF16)
    hid[x, 2] = (d_hidden * silu).astype(BF16)
    ag_step(1, 1)
    ag_step(2, 1)
    add_grad(x)

    def left(k):
        return lax.rem(x - k + nx, nx)

    def right(k):
        return lax.rem(x + k, nx)

    def send_back(side):
        for j in range(nj):
            rows_f[side, pl.ds(j, rows, stride=nj), :] = acc[side, :, j * LANES:(j + 1) * LANES]
        spread(side, 1)

    for k in range(2, hx + 1):
        ag_step(0, k)
        add_out(left(k - 1))
        add_out(right(k - 1))
        if k > 2:
            ag_step(1, k - 1)
            ag_step(2, k - 1)
            add_grad(left(k - 2))
            add_grad(right(k - 2))
    for direction in range(2):
        ag_copy(direction, hx, 0, True).wait_recv()
    add_out(right(hx))
    send_back(0)
    ag_step(1, hx)
    ag_step(2, hx)
    add_grad(left(hx - 1))
    add_grad(right(hx - 1))
    for m in (1, 2):
        for direction in range(2):
            ag_copy(direction, hx, m, True).wait_recv()
    add_grad(right(hx))
    send_back(1)

    def ys_copy(side, k, peer):
        return remote(ys.at[side, lax.rem(y + k, ny)], yr.at[side, peer], ys_sem, (side, k), y_dev(k))

    def xo_copy(side, k, peer):
        dest = lax.rem(x + k, nx)
        return remote(xo.at[side, dest], xi.at[side, peer], xo_sem, (side, k), x_dev(k))

    def home_rows(side):
        for j, part in enumerate(collect(1, side)):
            total = matmul(wsel_t[...], part)
            pf[j] = total
            ys[side, :, j] = total.astype(BF16).reshape(ny, block, LANES)
        each(1, ny, lambda k: ys_copy(side, k, y).start())

    def home_sum(side):
        each(1, ny, lambda k: ys_copy(side, k, lax.rem(y - k + ny, ny)).wait_recv())
        for j in range(nj):
            total = ps[side, j]
            for k in range(1, ny):
                total = total + yr[side, lax.rem(y + k, ny), j].astype(F32)
            final[pl.ds(j, block, stride=nj), :] = total
        xo[side] = final[...].reshape(nx, tok * nj, LANES)
        xi[side, pl.ds(x, 1)] = xo[side, pl.ds(x, 1)]
        each(1, nx, lambda k: xo_copy(side, k, x).start())

    def keep_own(side):
        for j in range(nj):
            ps[side, j] = pf[j, pl.ds(pl.multiple_of(y * block, 8), block), :]

    def finish(side, out):
        each(1, nx, lambda k: xo_copy(side, k, lax.rem(x - k + nx, nx)).wait_recv())
        whole = []
        for src in range(nx):
            got = xi[side, src]
            for j in range(nj):
                whole.append(jnp.concatenate([got[i * nj + j:i * nj + j + 1] for i in range(tok)], 0))
        out[...] = jnp.concatenate(whole, 1).astype(BF16)

    home_rows(0)
    keep_own(0)
    home_sum(0)
    home_rows(1)
    keep_own(1)
    home_sum(1)
    finish(0, mixed)
    finish(1, token_grad)

    each(1, nx, lambda k: x_copy(k, x).wait_send())
    for direction in range(2):
        for k in range(1, hy + 1):
            y_copy(direction, k).wait_send()
        for d in range(1, hx + 1):
            for m in range(3):
                rs_copy(direction, d, m).wait_send()
                ag_copy(direction, d, m).wait_send()
    for side in range(2):
        for way in range(2):
            each(1, ng, lambda k: z_copy(way, side, k, g).wait_send())
        each(1, ny, lambda k: ys_copy(side, k, y).wait_send())
        each(1, nx, lambda k: xo_copy(side, k, x).wait_send())


def per_device(nx, ny, ng, tokens, cotangent, gates, expert_ids, capacity, w_gate, w_up, w_down):
    tok, width = tokens.shape
    top = expert_ids.shape[1]
    w, ff = w_gate.shape
    experts = capacity.shape[0]
    block = nx * tok
    group = ny * block
    slots = min(group * top // experts * 5 // 4, group)
    rows = ng * slots
    nj = w // LANES
    ns = 2 * nj
    fc = ff // nx
    padded = -(-slots * nj // 16) * 16
    cap = capacity.reshape(1, experts)
    if experts < LANES:
        cap = jnp.pad(cap, ((0, 0), (0, LANES - experts)))
    vmem = pl.BlockSpec(memory_space=pltpu.VMEM)
    hbm = pl.BlockSpec(memory_space=pl.ANY)
    dma = pltpu.SemaphoreType.DMA
    return pl.pallas_call(
        functools.partial(moe_kernel, nx, ny, ng, slots),
        out_shape=[jax.ShapeDtypeStruct((tok, width), BF16)] * 2,
        in_specs=[vmem] * 5 + [hbm] * 3,
        out_specs=[vmem] * 2,
        scratch_shapes=[
            pltpu.VMEM((w, ff), BF16),
            pltpu.VMEM((w, ff), BF16),
            pltpu.VMEM((ff, w), BF16),
            pltpu.VMEM((tok, LANES), F32),
            pltpu.VMEM((nx, 2 * tok * ns, LANES), F32),
            pltpu.VMEM((nx, 2 * tok * ns, LANES), BF16),
            pltpu.VMEM((nx, 2 * tok * ns, LANES), BF16),
            pltpu.VMEM((2, nx * tok * ns, LANES), F32),
            pltpu.VMEM((ny, ns + 1, block, LANES), BF16),
            pltpu.VMEM((group, rows), BF16),
            pltpu.VMEM((4, rows * nj, LANES), F32),
            pltpu.VMEM((2, 2, ng, padded, LANES), BF16),
            pltpu.VMEM((2, 2, ng, padded, LANES), BF16),
            pltpu.VMEM((2, rows, w), BF16),
            pltpu.VMEM((2, nx // 2, 3, rows, fc), BF16),
            pltpu.VMEM((2, nx // 2, 3, rows, fc), BF16),
            pltpu.VMEM((nx, 3, rows, fc), BF16),
            pltpu.VMEM((2, rows, w), F32),
            pltpu.VMEM((2, nj, block, LANES), F32),
            pltpu.VMEM((nj, group, LANES), F32),
            pltpu.VMEM((2, ny, nj, block, LANES), BF16),
            pltpu.VMEM((2, ny, nj, block, LANES), BF16),
            pltpu.VMEM((2, nx, tok * nj, LANES), F32),
            pltpu.VMEM((2, nx, tok * nj, LANES), F32),
            pltpu.VMEM((block * nj, LANES), F32),
            dma((3,)),
            dma((2, nx)),
            dma((2, 2, ny // 2 + 1)),
            dma((2, 2, 2, ng)),
            dma((2, 2, nx // 2, 3)),
            dma((2, 2, nx // 2, 3)),
            dma((1,)),
            dma((2, 2, ny)),
            dma((2, 2, nx)),
        ],
        compiler_params=pltpu.CompilerParams(
            collective_id=0, has_side_effects=True, vmem_limit_bytes=40 * 1024 * 1024),
    )(tokens, cotangent, gates, expert_ids, cap, w_gate, w_up, w_down)


def solution(mesh):
    def run(tokens, cotangent, gates, expert_ids, capacity, w_gate, w_up, w_down):
        ng, local = mesh.shape["group"], mesh.shape["local"]
        w = w_gate.shape[0] // (ng * local)
        nx = tokens.shape[1] // w
        spec = P(("group", "local"), None)
        return jax.shard_map(
            functools.partial(per_device, nx, local // nx, ng),
            mesh=mesh,
            in_specs=(spec, spec, spec, spec, P(), spec, spec, P(None, ("group", "local"))),
            out_specs=(spec, spec),
            check_vma=False,
        )(tokens, cotangent, gates, expert_ids, capacity, w_gate, w_up, w_down)

    return run
```

```python
import functools

import jax
import jax.numpy as jnp
from jax import lax
from jax.experimental import pallas as pl
from jax.experimental.pallas import tpu as pltpu
from jax.sharding import PartitionSpec as P

LANES = 128
BF16 = jnp.bfloat16
F32 = jnp.float32
MESH = pl.DeviceIdType.MESH
CONTRACT_LAST = (((1,), (1,)), ((), ()))


def matmul(a, b):
    return jnp.dot(a, b, preferred_element_type=F32)


def matmul_t(a, b):
    return lax.dot_general(a, b, CONTRACT_LAST, preferred_element_type=F32)


def moe_kernel(
    nx, ny, ng, slots,
    tokens_hbm, cotangent_hbm, gates_hbm, ids_hbm, cap_hbm, wg_hbm, wu_hbm, wd_hbm,
    result,
    tokens, cotangent, gates, ids, cap, wg, wu, wd,
    meta_out, meta_in, xs_f, xs, xr, xf, wsel_t, rows_f, zs, zr, acts,
    far_out, far_in, three_out, three_in, one_out, one_in, two_out, two_in, hid, acc, ho_f, ho, hi,
    load_sem, x_sem, m_sem, z_sem, rs_sem, ag_sem, h_sem,
):
    tok, width = tokens.shape
    top = ids.shape[1]
    w = wg.shape[0]
    fc = wg.shape[1] // nx
    nj = w // LANES
    ns = 2 * nj
    nl = nx * ny
    group = nl * tok
    rows = ng * slots
    half = rows // 2
    used = slots * nj
    padded = zs.shape[3]
    hx = nx // 2

    g = lax.axis_index("group")
    at = lax.axis_index("local")
    y = lax.div(at, nx)
    x = lax.rem(at, nx)

    def x_dev(k):
        return {"local": y * nx + lax.rem(x + k + nx, nx)}

    def each(low, high, body):
        def step(i, carry):
            body(i)
            return carry
        lax.fori_loop(low, high, step, 0)

    def far_first(p, n):
        return n // 2 + (p + 1) // 2 * (1 - 2 * (p % 2))

    x_order = [far_first(q, nx) for q in range(nx)]
    x_places = [lax.rem(x + k, nx) for k in x_order]

    def each_local(body):
        def line(p):
            base = lax.rem(y + ny // 2 + lax.div(p + 1, 2) * (1 - 2 * lax.rem(p, 2)), ny) * nx
            for there in x_places:
                body(base + there, there)

        each(0, ny - 1, line)
        for there in x_places[:-1]:
            body(y * nx + there, there)

    def each_group(body):
        each(0, ng - 1, lambda p: body(lax.rem(g + ng // 2 + lax.div(p + 1, 2) * (1 - 2 * lax.rem(p, 2)), ng)))

    def remote(src, dst, sems, index, device):
        return pltpu.make_async_remote_copy(
            src_ref=src, dst_ref=dst, send_sem=sems.at[(0,) + index], recv_sem=sems.at[(1,) + index],
            device_id=device, device_id_type=MESH)

    def all_of(ref, count, sems, index):
        part = ref.at[pl.ds(0, count)]
        return remote(part, part, sems, index, x_dev(1))

    loads = [pltpu.make_async_copy(a, b, load_sem.at[i]) for i, (a, b) in enumerate((
        (tokens_hbm, tokens), (cotangent_hbm, cotangent), (gates_hbm, gates), (ids_hbm, ids),
        (cap_hbm, cap), (wg_hbm, wg), (wu_hbm, wu), (wd_hbm, wd)))]
    small, weights = loads[:5], loads[5:]
    for copy in loads:
        copy.start()

    barrier = pltpu.get_barrier_semaphore()

    def greet(device):
        pl.semaphore_signal(barrier, inc=1, device_id=device, device_id_type=MESH)

    each_local(lambda there, tx: greet({"local": there}))
    each_group(lambda there: greet({"group": there}))

    with jax.named_scope("cut_tokens"):
        for copy in small:
            copy.wait()
        meta_out[...] = jnp.zeros_like(meta_out)
        meta_out[0:tok, 0:top] = ids[...].astype(F32)
        meta_out[0:tok, top:2 * top] = gates[...].astype(F32)

        def cut(dest):
            start = pl.multiple_of(dest * w, LANES)
            for side, ref in enumerate((tokens, cotangent)):
                v = ref[:, pl.ds(start, w)].astype(F32)
                for i in range(tok):
                    for j in range(nj):
                        r = i * ns + side * nj + j
                        xs_f[dest, r:r + 1, :] = v[i:i + 1, j * LANES:(j + 1) * LANES]

        each(0, nx, cut)
        xs[...] = xs_f[...].astype(BF16)
        xr[pl.ds(at, 1)] = xs[pl.ds(x, 1)]
        meta_in[pl.ds(at, 1)] = meta_out[...].reshape(1, 8, LANES)

    with jax.named_scope("entry_wait"):
        pl.semaphore_wait(barrier, nl + ng - 2)

    def exchange(there, tx):
        remote(meta_out.at[pl.ds(0, tok)], meta_in.at[at, pl.ds(0, tok)], m_sem, (), {"local": there}).start()
        remote(xs.at[tx], xr.at[at], x_sem, (), {"local": there}).start()

    metas = all_of(meta_in.at[:, pl.ds(0, tok)], nl - 1, m_sem, ())
    blocks = all_of(xr, nl - 1, x_sem, ())

    with jax.named_scope("token_exchange"):
        each_local(exchange)
        metas.wait_recv()

    with jax.named_scope("routing"):
        xf[0:nl * 8] = meta_in[...].reshape(nl * 8, LANES)
        meta = jnp.concatenate([xf[pl.ds(i, nl, stride=8), :] for i in range(tok)], 0)
        expert = lax.broadcasted_iota(jnp.int32, (group, LANES), 1).astype(F32)
        hit = jnp.zeros((group, LANES), F32)
        weight = jnp.zeros((group, LANES), F32)
        for k in range(top):
            same = meta[:, k:k + 1] == expert
            hit = jnp.where(same, 1.0, hit)
            weight = jnp.where(same, meta[:, top + k:top + k + 1], weight)

        def order(axis):
            p = lax.broadcasted_iota(jnp.int32, (group, group), axis)
            turn = jnp.where(p >= nl, 1, 0)
            for i in range(2, tok):
                turn = jnp.where(p >= i * nl, i, turn)
            return (p - turn * nl) * tok + turn

        earlier = order(1) < order(0)
        rank = matmul(jnp.where(earlier, 1.0, 0.0).astype(BF16), hit.astype(BF16))
        kept = (hit > 0.5) & (rank < cap[...].astype(F32))
        rank = jnp.where(kept, rank, -1.0).astype(BF16)
        weight = weight.astype(BF16)

        r_group = jnp.floor((lax.broadcasted_iota(jnp.int32, (rows, LANES), 0).astype(F32) + 0.5) * (1.0 / slots))
        r_expert = r_group * ny + y.astype(F32)
        pick = jnp.where(lax.broadcasted_iota(jnp.int32, (rows, LANES), 1).astype(F32) == r_expert, 1.0, 0.0).astype(BF16)
        r_at = lax.broadcasted_iota(jnp.int32, (rows, group), 0).astype(F32)
        r_slot = r_at - jnp.floor((r_at + 0.5) * (1.0 / slots)) * slots
        select = jnp.where(matmul_t(pick, rank) == r_slot, 1.0, 0.0).astype(BF16)
        c_at = lax.broadcasted_iota(jnp.int32, (group, rows), 1).astype(F32)
        c_slot = c_at - jnp.floor((c_at + 0.5) * (1.0 / slots)) * slots
        wsel_t[...] = jnp.where(matmul_t(rank, pick) == c_slot, matmul_t(weight, pick), 0.0).astype(BF16)

    def row_blocks(way, side):
        return all_of(zr.at[way, side], ng - 1, z_sem, (way, side))

    def spread(side, way):
        def part_of(dest):
            part = rows_f[side, pl.ds(pl.multiple_of(dest * used, 8), used), :]
            if padded > used:
                part = jnp.concatenate([part, jnp.zeros((padded - used, LANES), F32)], 0)
            return part.astype(BF16)

        def go(dest):
            zs[way, side, dest] = part_of(dest)
            remote(zs.at[way, side, dest], zr.at[way, side, g], z_sem, (way, side), {"group": dest}).start()

        each_group(go)
        zr[way, side, g] = part_of(g)

    def collect(way, side):
        row_blocks(way, side).wait_recv()
        got = zr[way, side].astype(F32)
        rows_f[2 + side] = got[:, 0:used].reshape(ng * used, LANES)
        return [rows_f[2 + side, pl.ds(j, rows, stride=nj), :].astype(BF16) for j in range(nj)]

    with jax.named_scope("token_wait"):
        blocks.wait_recv()

    with jax.named_scope("row_send"):
        xf[...] = xr[...].astype(F32).reshape(nl * tok * ns, LANES)
        for side in range(2):
            for j in range(nj):
                held = jnp.concatenate(
                    [xf[pl.ds(i * ns + side * nj + j, nl, stride=tok * ns), :] for i in range(tok)], 0).astype(BF16)
                rows_f[side, pl.ds(j, rows, stride=nj), :] = matmul(select, held)
            spread(side, 0)

    def lanes_of(chunk):
        return pl.ds(pl.multiple_of(chunk * fc, LANES), fc)

    def products(kind, chunk):
        here = lanes_of(chunk)
        if kind == 0:
            both = matmul(acts[0], jnp.concatenate([wg[:, here], wu[:, here]], 1))
            return [(0, both[:, 0:fc]), (1, both[:, fc:2 * fc])]
        return [(2, matmul_t(acts[1], wd[here, :]))]

    def chunk_at(k):
        return lax.rem(x + k + nx, nx)

    FAR, THREE, ONE, TWO = range(4)
    routes = {FAR: (far_out, far_in, 2), THREE: (three_out, three_in, 1), ONE: (one_out, one_in, 1),
              TWO: (two_out, two_in, 2)}
    signs = (1, -1)

    def rs_copy(route, way, m):
        out, into, distance = routes[route]
        return remote(out.at[way, m], into.at[way, m], rs_sem, (route, way, m), x_dev(signs[way] * distance))

    def rs_far(kind):
        for m, part in products(kind, chunk_at(hx)):
            for way in range(2):
                far_out[way, m] = (part[0:half] if way == 0 else part[half:rows]).astype(BF16)
                rs_copy(FAR, way, m).start()

    def rs_plain(kind, route, distance):
        out = routes[route][0]
        for way in range(2):
            for m, part in products(kind, chunk_at(signs[way] * distance)):
                out[way, m] = part.astype(BF16)
                rs_copy(route, way, m).start()

    def rs_pass(kind):
        for way in range(2):
            for m, part in products(kind, chunk_at(signs[way] * 2)):
                rs_copy(FAR, way, m).wait_recv()
                rs_copy(THREE, way, m).wait_recv()
                part = part + three_in[way, m].astype(F32)
                add = far_in[way, m].astype(F32)
                if way == 0:
                    two_out[way, m, 0:half] = (part[0:half] + add).astype(BF16)
                    two_out[way, m, half:rows] = part[half:rows].astype(BF16)
                else:
                    two_out[way, m, 0:half] = part[0:half].astype(BF16)
                    two_out[way, m, half:rows] = (part[half:rows] + add).astype(BF16)
                rs_copy(TWO, way, m).start()

    def rs_last(kind):
        totals = []
        for m, part in products(kind, x):
            for route, ref in ((ONE, one_in), (TWO, two_in)):
                for way in range(2):
                    rs_copy(route, way, m).wait_recv()
                    part = part + ref[way, m].astype(F32)
            totals.append(part)
        return totals

    def ag_copy(way, distance, m, receive=False):
        back = distance if receive else (0 if distance <= 2 else 2)
        ref = hid.at[chunk_at(-signs[way] * back), m]
        if distance == hx:
            ref = ref.at[pl.ds(0, half)] if way == 0 else ref.at[pl.ds(half, rows - half)]
        hop = distance if distance <= 2 else distance - 2
        return remote(ref, ref, ag_sem, (way, distance - 1, m), x_dev(signs[way] * hop))

    def ag_start(m):
        for distance in (2, 1):
            for way in range(2):
                ag_copy(way, distance, m).start()

    def ag_pass(m):
        for way in range(2):
            ag_copy(way, 2, m, True).wait_recv()
            for distance in range(hx, 2, -1):
                ag_copy(way, distance, m).start()

    def ag_wait(m, distance):
        for way in range(2):
            ag_copy(way, distance, m, True).wait_recv()

    def add_out(chunk):
        acc[0] += matmul(hid[chunk, 0], wd[lanes_of(chunk), :])

    def add_grad(chunk):
        here = lanes_of(chunk)
        acc[1] += matmul_t(jnp.concatenate([hid[chunk, 1], hid[chunk, 2]], 1),
                           jnp.concatenate([wg[:, here], wu[:, here]], 1))

    def both_sides(add, distance):
        add(chunk_at(distance))
        add(chunk_at(-distance))

    with jax.named_scope("rows_wait"):
        for j, part in enumerate(collect(0, 0)):
            acts[0, :, j * LANES:(j + 1) * LANES] = part
        for copy in weights:
            copy.wait()

    with jax.named_scope("gate_up_start"):
        rs_far(0)
        rs_plain(0, THREE, 3)
        rs_plain(0, ONE, 1)

    with jax.named_scope("cotangent_wait"):
        for j, part in enumerate(collect(0, 1)):
            acts[1, :, j * LANES:(j + 1) * LANES] = part

    with jax.named_scope("back_start"):
        rs_far(1)
        rs_plain(1, THREE, 3)

    with jax.named_scope("gate_up_pass"):
        rs_pass(0)

    with jax.named_scope("back_pass"):
        rs_plain(1, ONE, 1)
        rs_pass(1)

    with jax.named_scope("gate_up_last"):
        gate_pre, up_pre = rs_last(0)
        sig = jax.nn.sigmoid(gate_pre)
        silu = gate_pre * sig
        hid[x, 0] = (silu * up_pre).astype(BF16)
        ag_start(0)
        d_gate_by = up_pre * sig * (1.0 + gate_pre * (1.0 - sig))

    with jax.named_scope("back_last"):
        acc[...] = jnp.zeros_like(acc)
        add_out(x)
        (d_hidden,) = rs_last(1)
        hid[x, 1] = (d_hidden * d_gate_by).astype(BF16)
        ag_start(1)
        hid[x, 2] = (d_hidden * silu).astype(BF16)
        ag_start(2)

    with jax.named_scope("hidden_pass"):
        add_grad(x)
        ag_pass(0)
        ag_wait(0, 1)
        both_sides(add_out, 1)
        both_sides(add_out, 2)

    with jax.named_scope("grad_pass"):
        ag_pass(1)
        ag_pass(2)

    with jax.named_scope("out_rest"):
        for distance in range(3, hx):
            ag_wait(0, distance)
            both_sides(add_out, distance)
        ag_wait(0, hx)
        add_out(chunk_at(hx))

    def send_back(side):
        for j in range(nj):
            rows_f[side, pl.ds(j, rows, stride=nj), :] = acc[side, :, j * LANES:(j + 1) * LANES]
        spread(side, 1)

    with jax.named_scope("out_send"):
        send_back(0)

    with jax.named_scope("grad_rest"):
        for m in (1, 2):
            ag_wait(m, 1)
        both_sides(add_grad, 1)
        both_sides(add_grad, 2)
        for distance in range(3, hx):
            for m in (1, 2):
                ag_wait(m, distance)
            both_sides(add_grad, distance)
        for m in (1, 2):
            ag_wait(m, hx)
        add_grad(chunk_at(hx))

    with jax.named_scope("grad_send"):
        send_back(1)

    mine = tok * ns
    sums = all_of(hi, nl - 1, h_sem, ())

    def weigh(side):
        for j, part in enumerate(collect(1, side)):
            total = matmul(wsel_t[...], part)
            for i in range(tok):
                ho_f[pl.ds((side * tok + i) * nj + j, nl, stride=mine), :] = total[i * nl:(i + 1) * nl]

    def send_home(there, tx):
        remote(ho.at[there], hi.at[at], h_sem, (), {"local": there}).start()

    with jax.named_scope("mixed_rows"):
        weigh(0)

    with jax.named_scope("grad_rows"):
        weigh(1)

    with jax.named_scope("home_send"):
        ho[...] = ho_f[...].astype(BF16).reshape(nl, mine, LANES)
        each_local(send_home)
        hi[pl.ds(at, 1)] = ho[pl.ds(at, 1)]

    with jax.named_scope("home_wait"):
        sums.wait_recv()

    with jax.named_scope("finish"):
        total = jnp.sum(hi[...].astype(F32).reshape(ny, nx, mine, LANES), axis=0)
        whole = []
        for src in range(nx):
            for j in range(nj):
                whole.append(jnp.concatenate([total[src, i * nj + j:i * nj + j + 1] for i in range(2 * tok)], 0))
        result[...] = jnp.concatenate(whole, 1)

    with jax.named_scope("drain"):
        metas.wait_send()
        blocks.wait_send()
        sums.wait_send()
        for side in range(2):
            for way in range(2):
                row_blocks(way, side).wait_send()
        for way in range(2):
            for m in range(3):
                for route in routes:
                    rs_copy(route, way, m).wait_send()
                for distance in range(1, hx + 1):
                    ag_copy(way, distance, m).wait_send()


def per_device(nx, ny, ng, tokens, cotangent, gates, expert_ids, capacity, w_gate, w_up, w_down):
    tok, width = tokens.shape
    top = expert_ids.shape[1]
    w, ff = w_gate.shape
    experts = capacity.shape[0]
    nl = nx * ny
    group = nl * tok
    slots = min(group * top // experts * 5 // 4, group)
    rows = ng * slots
    nj = w // LANES
    ns = 2 * nj
    fc = ff // nx
    padded = -(-slots * nj // 16) * 16
    cap = capacity.reshape(1, experts)
    if experts < LANES:
        cap = jnp.pad(cap, ((0, 0), (0, LANES - experts)))
    vmem = pl.BlockSpec(memory_space=pltpu.VMEM)
    hbm = pl.BlockSpec(memory_space=pl.ANY)
    dma = pltpu.SemaphoreType.DMA
    both = pl.pallas_call(
        functools.partial(moe_kernel, nx, ny, ng, slots),
        out_shape=jax.ShapeDtypeStruct((2 * tok, width), F32),
        in_specs=[hbm] * 8,
        out_specs=vmem,
        scratch_shapes=[
            pltpu.VMEM((tok, width), BF16),
            pltpu.VMEM((tok, width), BF16),
            pltpu.VMEM((tok, top), BF16),
            pltpu.VMEM((tok, top), jnp.int32),
            pltpu.VMEM(cap.shape, jnp.int32),
            pltpu.VMEM((w, ff), BF16),
            pltpu.VMEM((w, ff), BF16),
            pltpu.VMEM((ff, w), BF16),
            pltpu.VMEM((8, LANES), F32),
            pltpu.VMEM((nl, 8, LANES), F32),
            pltpu.VMEM((nx, tok * ns, LANES), F32),
            pltpu.VMEM((nx, tok * ns, LANES), BF16),
            pltpu.VMEM((nl, tok * ns, LANES), BF16),
            pltpu.VMEM((nl * tok * ns, LANES), F32),
            pltpu.VMEM((group, rows), BF16),
            pltpu.VMEM((4, rows * nj, LANES), F32),
            pltpu.VMEM((2, 2, ng, padded, LANES), BF16),
            pltpu.VMEM((2, 2, ng, padded, LANES), BF16),
            pltpu.VMEM((2, rows, w), BF16),
            pltpu.VMEM((2, 3, rows // 2, fc), BF16),
            pltpu.VMEM((2, 3, rows // 2, fc), BF16),
        ] + [pltpu.VMEM((2, 3, rows, fc), BF16)] * 6 + [
            pltpu.VMEM((nx, 3, rows, fc), BF16),
            pltpu.VMEM((2, rows, w), F32),
            pltpu.VMEM((nl * tok * ns, LANES), F32),
            pltpu.VMEM((nl, tok * ns, LANES), BF16),
            pltpu.VMEM((nl, tok * ns, LANES), BF16),
            dma((8,)),
            dma((2,)),
            dma((2,)),
            dma((2, 2, 2)),
            dma((2, 4, 2, 3)),
            dma((2, 2, nx // 2, 3)),
            dma((2,)),
        ],
        compiler_params=pltpu.CompilerParams(
            collective_id=0, has_side_effects=True, vmem_limit_bytes=60 * 1024 * 1024),
    )(tokens, cotangent, gates, expert_ids, cap, w_gate, w_up, w_down)
    return both[:tok].astype(BF16), both[tok:].astype(BF16)


def solution(mesh):
    def run(tokens, cotangent, gates, expert_ids, capacity, w_gate, w_up, w_down):
        ng, local = mesh.shape["group"], mesh.shape["local"]
        w = w_gate.shape[0] // (ng * local)
        nx = tokens.shape[1] // w
        spec = P(("group", "local"), None)
        return jax.shard_map(
            functools.partial(per_device, nx, local // nx, ng),
            mesh=mesh,
            in_specs=(spec, spec, spec, spec, P(), spec, spec, P(None, ("group", "local"))),
            out_specs=(spec, spec),
            check_vma=False,
        )(tokens, cotangent, gates, expert_ids, capacity, w_gate, w_up, w_down)

    return run
```

```python
import functools

import jax
import jax.numpy as jnp
from jax import lax
from jax.experimental import pallas as pl
from jax.experimental.pallas import tpu as pltpu
from jax.sharding import PartitionSpec as P

LANES = 128
BF16 = jnp.bfloat16
F32 = jnp.float32
MESH = pl.DeviceIdType.MESH
CONTRACT_LAST = (((1,), (1,)), ((), ()))


def matmul(a, b):
    return jnp.dot(a, b, preferred_element_type=F32)


def matmul_t(a, b):
    return lax.dot_general(a, b, CONTRACT_LAST, preferred_element_type=F32)


def pieces(used):
    return -(-used // 16) * 16, used // 16 * 16


def moe_kernel(
    nx, ny, ng, slots,
    tokens_hbm, cotangent_hbm, gates_hbm, ids_hbm, cap_hbm, wg_hbm, wu_hbm, wd_hbm,
    result,
    tokens, cotangent, gates, ids, cap, wg, wu, wd,
    meta_out, meta_in, xs_f, xs, xr, xf, wsel_t, rows_f, zs, zr, acts,
    far_out, far_in, three_out, three_in, one_out, one_in, two_out, two_in, hid, acc, ho_f, ho, hi,
    load_sem, x_sem, m_sem, z_sem, rs_sem, ag_sem, sent_sem, h_sem,
):
    tok, width = tokens.shape
    top = ids.shape[1]
    w = wg.shape[0]
    fc = wg.shape[1] // nx
    nj = w // LANES
    ns = 2 * nj
    nl = nx * ny
    group = nl * tok
    rows = ng * slots
    part_rows = rows // 2
    top_rows = far_out.shape[3]
    used = slots * nj
    cuts = pieces(used)
    hx = nx // 2

    g = lax.axis_index("group")
    at = lax.axis_index("local")
    y = lax.div(at, nx)
    x = lax.rem(at, nx)

    def x_dev(k):
        return {"local": y * nx + lax.rem(x + k + nx, nx)}

    def each(low, high, body):
        def step(i, carry):
            body(i)
            return carry
        lax.fori_loop(low, high, step, 0)

    def far_first(p, n):
        return n // 2 + (p + 1) // 2 * (1 - 2 * (p % 2))

    x_order = [far_first(q, nx) for q in range(nx)]
    x_places = [lax.rem(x + k, nx) for k in x_order]

    def each_local(body):
        def line(p):
            base = lax.rem(y + ny // 2 + lax.div(p + 1, 2) * (1 - 2 * lax.rem(p, 2)), ny) * nx
            for there in x_places:
                body(base + there, there)

        each(0, ny - 1, line)
        for there in x_places[:-1]:
            body(y * nx + there, there)

    def each_group(body):
        each(0, ng - 1, lambda p: body(lax.rem(g + ng // 2 + lax.div(p + 1, 2) * (1 - 2 * lax.rem(p, 2)), ng)))

    def remote(src, dst, sems, index, device):
        return pltpu.make_async_remote_copy(
            src_ref=src, dst_ref=dst, send_sem=sems.at[(0,) + index], recv_sem=sems.at[(1,) + index],
            device_id=device, device_id_type=MESH)

    def all_of(ref, count, sems, index):
        part = ref.at[pl.ds(0, count)]
        return remote(part, part, sems, index, x_dev(1))

    loads = [pltpu.make_async_copy(a, b, load_sem.at[i]) for i, (a, b) in enumerate((
        (tokens_hbm, tokens), (cotangent_hbm, cotangent), (gates_hbm, gates), (ids_hbm, ids),
        (cap_hbm, cap), (wg_hbm, wg), (wu_hbm, wu), (wd_hbm, wd)))]
    small, weights = loads[:5], loads[5:]

    barrier = pltpu.get_barrier_semaphore()

    def greet(device):
        pl.semaphore_signal(barrier, inc=1, device_id=device, device_id_type=MESH)

    each_local(lambda there, tx: greet({"local": there}))
    each_group(lambda there: greet({"group": there}))
    for copy in loads:
        copy.start()

    with jax.named_scope("cut_tokens"):
        for copy in small:
            copy.wait()
        meta_out[...] = jnp.zeros_like(meta_out)
        meta_out[0:tok, 0:top] = ids[...].astype(F32)
        meta_out[0:tok, top:2 * top] = gates[...].astype(F32)

        def cut(dest):
            start = pl.multiple_of(dest * w, LANES)
            for side, ref in enumerate((tokens, cotangent)):
                v = ref[:, pl.ds(start, w)].astype(F32)
                for i in range(tok):
                    for j in range(nj):
                        r = i * ns + side * nj + j
                        xs_f[dest, r:r + 1, :] = v[i:i + 1, j * LANES:(j + 1) * LANES]

        each(0, nx, cut)
        xs[...] = xs_f[...].astype(BF16)
        xr[pl.ds(at, 1)] = xs[pl.ds(x, 1)]
        meta_in[pl.ds(at, 1)] = meta_out[...].reshape(1, 8, LANES)

    with jax.named_scope("entry_wait"):
        pl.semaphore_wait(barrier, nl + ng - 2)

    def exchange(there, tx):
        remote(meta_out.at[pl.ds(0, tok)], meta_in.at[at, pl.ds(0, tok)], m_sem, (), {"local": there}).start()
        remote(xs.at[tx], xr.at[at], x_sem, (), {"local": there}).start()

    metas = all_of(meta_in.at[:, pl.ds(0, tok)], nl - 1, m_sem, ())
    blocks = all_of(xr, nl - 1, x_sem, ())

    with jax.named_scope("token_exchange"):
        each_local(exchange)
        metas.wait_recv()

    with jax.named_scope("routing"):
        xf[0:nl * 8] = meta_in[...].reshape(nl * 8, LANES)
        meta = jnp.concatenate([xf[pl.ds(i, nl, stride=8), :] for i in range(tok)], 0)
        expert = lax.broadcasted_iota(jnp.int32, (group, LANES), 1).astype(F32)
        hit = jnp.zeros((group, LANES), F32)
        weight = jnp.zeros((group, LANES), F32)
        for k in range(top):
            same = meta[:, k:k + 1] == expert
            hit = jnp.where(same, 1.0, hit)
            weight = jnp.where(same, meta[:, top + k:top + k + 1], weight)

        def order(axis):
            p = lax.broadcasted_iota(jnp.int32, (group, group), axis)
            turn = jnp.where(p >= nl, 1, 0)
            for i in range(2, tok):
                turn = jnp.where(p >= i * nl, i, turn)
            return (p - turn * nl) * tok + turn

        earlier = order(1) < order(0)
        rank = matmul(jnp.where(earlier, 1.0, 0.0).astype(BF16), hit.astype(BF16))
        kept = (hit > 0.5) & (rank < cap[...].astype(F32))
        rank = jnp.where(kept, rank, -1.0).astype(BF16)
        weight = weight.astype(BF16)

        r_group = jnp.floor((lax.broadcasted_iota(jnp.int32, (rows, LANES), 0).astype(F32) + 0.5) * (1.0 / slots))
        r_expert = r_group * ny + y.astype(F32)
        pick = jnp.where(lax.broadcasted_iota(jnp.int32, (rows, LANES), 1).astype(F32) == r_expert, 1.0, 0.0).astype(BF16)
        r_at = lax.broadcasted_iota(jnp.int32, (rows, group), 0).astype(F32)
        r_slot = r_at - jnp.floor((r_at + 0.5) * (1.0 / slots)) * slots
        select = jnp.where(matmul_t(pick, rank) == r_slot, 1.0, 0.0).astype(BF16)
        c_at = lax.broadcasted_iota(jnp.int32, (group, rows), 1).astype(F32)
        c_slot = c_at - jnp.floor((c_at + 0.5) * (1.0 / slots)) * slots
        wsel_t[...] = jnp.where(matmul_t(rank, pick) == c_slot, matmul_t(weight, pick), 0.0).astype(BF16)

    def piece(way, index):
        low, high = (0, cuts[way]) if index == 0 else (cuts[way], 2 * used)
        return pl.ds(low, high - low)

    def row_blocks(way, index):
        return all_of(zr.at[way, :, piece(way, index)], ng - 1, z_sem, (way, index))

    def spread(way, index):
        low, high = (0, cuts[way]) if index == 0 else (cuts[way], 2 * used)
        here = piece(way, index)

        def part_of(dest):
            start = pl.multiple_of(dest * used, 8)
            parts = []
            if low < used:
                parts.append(rows_f[0, pl.ds(start + low, min(high, used) - low), :])
            if high > used:
                first = max(low, used)
                parts.append(rows_f[1, pl.ds(start + first - used, high - first), :])
            return jnp.concatenate(parts, 0).astype(BF16)

        def go(dest):
            zs[way, dest, here] = part_of(dest)
            remote(zs.at[way, dest, here], zr.at[way, g, here], z_sem, (way, index), {"group": dest}).start()

        each_group(go)
        zr[way, g, here] = part_of(g)

    def lay_out(side, got):
        rows_f[2 + side] = got.astype(F32).reshape(ng * used, LANES)
        return [rows_f[2 + side, pl.ds(j, rows, stride=nj), :].astype(BF16) for j in range(nj)]

    with jax.named_scope("token_wait"):
        blocks.wait_recv()

    with jax.named_scope("row_send"):
        xf[...] = xr[...].astype(F32).reshape(nl * tok * ns, LANES)
        for side in range(2):
            for j in range(nj):
                held = jnp.concatenate(
                    [xf[pl.ds(i * ns + side * nj + j, nl, stride=tok * ns), :] for i in range(tok)], 0).astype(BF16)
                rows_f[side, pl.ds(j, rows, stride=nj), :] = matmul(select, held)
        spread(0, 0)
        spread(0, 1)

    def lanes_of(chunk):
        return pl.ds(pl.multiple_of(chunk * fc, LANES), fc)

    def of(part):
        return pl.ds(part * part_rows, part_rows)

    def products(kind, part, chunk):
        here = lanes_of(chunk)
        if kind == 0:
            both = matmul(acts[0, of(part)], jnp.concatenate([wg[:, here], wu[:, here]], 1))
            return [(0, both[:, 0:fc]), (1, both[:, fc:2 * fc])]
        return [(2, matmul_t(acts[1, of(part)], wd[here, :]))]

    def chunk_at(k):
        return lax.rem(x + k + nx, nx)

    FAR, THREE, TWO, ONE = range(4)
    routes = {FAR: (far_out, far_in, 2), THREE: (three_out, three_in, 1), TWO: (two_out, two_in, 1),
              ONE: (one_out, one_in, 1)}
    signs = (1, -1)
    rs_kinds = (pl.ds(0, 2), pl.ds(2, 1))
    ag_kinds = (pl.ds(0, 1), pl.ds(1, 2))

    def far_span(part, way):
        cut = top_rows if part == 0 else part_rows - top_rows
        return (0, cut) if way == 0 else (cut, part_rows)

    def one_way(src, dst, send_sem, recv_sem, device):
        return pltpu.make_async_remote_copy(
            src_ref=src, dst_ref=dst, send_sem=send_sem, recv_sem=recv_sem, device_id=device, device_id_type=MESH)

    def rs_copy(route, way, kind, part):
        out, into, distance = routes[route]
        out, into = out.at[part, way, rs_kinds[kind]], into.at[part, way, rs_kinds[kind]]
        if route == FAR:
            low, high = far_span(part, way)
            out, into = out.at[:, pl.ds(0, high - low)], into.at[:, pl.ds(0, high - low)]
        return one_way(out, into, sent_sem.at[0, part], rs_sem.at[route, way, kind, part], x_dev(signs[way] * distance))

    def rs_start(kind, part):
        shared = products(kind, part, chunk_at(hx))
        for way in range(2):
            low, high = far_span(part, way)
            for m, value in shared:
                far_out[part, way, m, 0:high - low] = value[low:high].astype(BF16)
            rs_copy(FAR, way, kind, part).start()
        for way in range(2):
            for m, value in products(kind, part, chunk_at(signs[way] * 3)):
                three_out[part, way, m] = value.astype(BF16)
            rs_copy(THREE, way, kind, part).start()

    def rs_two(kind, part):
        for way in range(2):
            mine = products(kind, part, chunk_at(signs[way] * 2))
            rs_copy(FAR, way, kind, part).wait_recv()
            rs_copy(THREE, way, kind, part).wait_recv()
            low, high = far_span(part, way)
            for m, value in mine:
                value = value + three_in[part, way, m].astype(F32)
                add = value[low:high] + far_in[part, way, m, 0:high - low].astype(F32)
                two_out[part, way, m, low:high] = add.astype(BF16)
                if way == 0:
                    two_out[part, way, m, high:part_rows] = value[high:part_rows].astype(BF16)
                else:
                    two_out[part, way, m, 0:low] = value[0:low].astype(BF16)
            rs_copy(TWO, way, kind, part).start()

    def rs_one(kind, part):
        for way in range(2):
            mine = products(kind, part, chunk_at(signs[way]))
            rs_copy(TWO, way, kind, part).wait_recv()
            for m, value in mine:
                one_out[part, way, m] = (value + two_in[part, way, m].astype(F32)).astype(BF16)
            rs_copy(ONE, way, kind, part).start()

    def rs_last(kind, part):
        mine = products(kind, part, x)
        for way in range(2):
            rs_copy(ONE, way, kind, part).wait_recv()
        return [value + (one_in[part, 0, m].astype(F32) + one_in[part, 1, m].astype(F32)) for m, value in mine]

    def ag_copy(way, distance, kind, part, receive=False):
        back = distance if receive else min(distance - 1, 2)
        ref = hid.at[part, chunk_at(-signs[way] * back), ag_kinds[kind]]
        if distance == hx:
            low, high = far_span(part, way)
            ref = ref.at[:, pl.ds(low, high - low)]
        hop = distance - min(distance - 1, 2)
        return one_way(ref, ref, sent_sem.at[1, part], ag_sem.at[way, distance - 1, kind, part], x_dev(signs[way] * hop))

    def ag_start(kind, part):
        for way in range(2):
            ag_copy(way, 1, kind, part).start()

    def ag_pass(kind, part, distance):
        for way in range(2):
            ag_copy(way, distance, kind, part, True).wait_recv()
            for further in (2,) if distance == 1 else range(hx, 2, -1):
                ag_copy(way, further, kind, part).start()

    def ag_wait(kind, part, distance):
        for way in range(2):
            ag_copy(way, distance, kind, part, True).wait_recv()

    def add_out(part, k):
        chunk = chunk_at(k)
        acc[0, of(part)] += matmul(hid[part, chunk, 0], wd[lanes_of(chunk), :])

    def add_grad(part, k):
        chunk = chunk_at(k)
        here = lanes_of(chunk)
        acc[1, of(part)] += matmul_t(jnp.concatenate([hid[part, chunk, 1], hid[part, chunk, 2]], 1),
                                     jnp.concatenate([wg[:, here], wu[:, here]], 1))

    adds = (add_out, add_grad)

    def add_both(kind, part, distance):
        adds[kind](part, distance)
        adds[kind](part, -distance)

    def add_rest(kind):
        for distance in range(3, hx):
            for part in range(2):
                ag_wait(kind, part, distance)
                add_both(kind, part, distance)
        for part in range(2):
            ag_wait(kind, part, hx)
            adds[kind](part, hx)

    with jax.named_scope("rows_wait"):
        row_blocks(0, 0).wait_recv()
        for j, part in enumerate(lay_out(0, zr[0, :, 0:cuts[0]].astype(F32)[:, 0:used])):
            acts[0, :, j * LANES:(j + 1) * LANES] = part
        for copy in weights:
            copy.wait()

    with jax.named_scope("gate_up_start"):
        for part in range(2):
            rs_start(0, part)

    with jax.named_scope("cotangent_wait"):
        row_blocks(0, 1).wait_recv()
        for j, part in enumerate(lay_out(1, zr[0].astype(F32)[:, used:2 * used])):
            acts[1, :, j * LANES:(j + 1) * LANES] = part

    with jax.named_scope("back_start"):
        for part in range(2):
            rs_start(1, part)

    with jax.named_scope("gate_up_two"):
        for part in range(2):
            rs_two(0, part)

    with jax.named_scope("back_two"):
        for part in range(2):
            rs_two(1, part)

    with jax.named_scope("gate_up_one"):
        for part in range(2):
            rs_one(0, part)

    with jax.named_scope("back_one"):
        acc[...] = jnp.zeros_like(acc)
        for part in range(2):
            rs_one(1, part)

    with jax.named_scope("gate_up_last"):
        saved = []
        for part in range(2):
            gate_pre, up_pre = rs_last(0, part)
            sig = jax.nn.sigmoid(gate_pre)
            silu = gate_pre * sig
            hid[part, x, 0] = (silu * up_pre).astype(BF16)
            ag_start(0, part)
            saved.append((up_pre * sig * (1.0 + gate_pre * (1.0 - sig)), silu))

    with jax.named_scope("back_last"):
        for part in range(2):
            (d_hidden,) = rs_last(1, part)
            hid[part, x, 1] = (d_hidden * saved[part][0]).astype(BF16)
            hid[part, x, 2] = (d_hidden * saved[part][1]).astype(BF16)
            ag_start(1, part)

    with jax.named_scope("hidden_pass_one"):
        for part in range(2):
            add_out(part, 0)
            ag_pass(0, part, 1)

    with jax.named_scope("grad_pass_one"):
        for part in range(2):
            add_grad(part, 0)
            ag_pass(1, part, 1)

    with jax.named_scope("hidden_pass_two"):
        for part in range(2):
            add_both(0, part, 1)
            ag_pass(0, part, 2)

    with jax.named_scope("grad_pass_two"):
        for part in range(2):
            add_both(1, part, 1)
            ag_pass(1, part, 2)

    with jax.named_scope("out_rest"):
        for part in range(2):
            add_both(0, part, 2)
        add_rest(0)

    def send_back(side):
        for j in range(nj):
            rows_f[side, pl.ds(j, rows, stride=nj), :] = acc[side, :, j * LANES:(j + 1) * LANES]
        spread(1, side)

    with jax.named_scope("out_send"):
        send_back(0)

    with jax.named_scope("grad_rest"):
        for part in range(2):
            add_both(1, part, 2)
        add_rest(1)

    with jax.named_scope("grad_send"):
        send_back(1)

    mine = tok * ns
    sums = all_of(hi, nl - 1, h_sem, ())

    def weigh(side):
        for j, part in enumerate(lay_out(side, zr[1].astype(F32)[:, side * used:(side + 1) * used])):
            total = matmul(wsel_t[...], part)
            for i in range(tok):
                ho_f[pl.ds((side * tok + i) * nj + j, nl, stride=mine), :] = total[i * nl:(i + 1) * nl]

    def send_home(there, tx):
        remote(ho.at[there], hi.at[at], h_sem, (), {"local": there}).start()

    with jax.named_scope("back_wait"):
        for index in range(2):
            row_blocks(1, index).wait_recv()

    with jax.named_scope("grad_rows"):
        for side in range(2):
            weigh(side)

    with jax.named_scope("home_send"):
        ho[...] = ho_f[...].astype(BF16).reshape(nl, mine, LANES)
        each_local(send_home)
        hi[pl.ds(at, 1)] = ho[pl.ds(at, 1)]

    with jax.named_scope("home_wait"):
        sums.wait_recv()

    with jax.named_scope("finish"):
        total = jnp.sum(hi[...].astype(F32).reshape(ny, nx, mine, LANES), axis=0)
        whole = []
        for src in range(nx):
            for j in range(nj):
                whole.append(jnp.concatenate([total[src, i * nj + j:i * nj + j + 1] for i in range(2 * tok)], 0))
        result[...] = jnp.concatenate(whole, 1).astype(BF16)

    with jax.named_scope("drain"):
        metas.wait_send()
        blocks.wait_send()
        sums.wait_send()
        for index in range(2):
            for way in range(2):
                row_blocks(way, index).wait_send()
        for stage in range(2):
            for part in range(2):
                chunks = hid.at[part, pl.ds(0, nx - 1)]
                one_way(chunks, chunks, sent_sem.at[stage, part], rs_sem.at[0, 0, 0, 0], x_dev(1)).wait_send()


def per_device(nx, ny, ng, tokens, cotangent, gates, expert_ids, capacity, w_gate, w_up, w_down):
    tok, width = tokens.shape
    top = expert_ids.shape[1]
    w, ff = w_gate.shape
    experts = capacity.shape[0]
    nl = nx * ny
    group = nl * tok
    slots = min(group * top // experts * 5 // 4, group)
    rows = ng * slots
    nj = w // LANES
    ns = 2 * nj
    fc = ff // nx
    part_rows = rows // 2
    top_rows = -(-part_rows // 32) * 16
    if top_rows >= part_rows:
        top_rows = part_rows // 2
    cap = capacity.reshape(1, experts)
    if experts < LANES:
        cap = jnp.pad(cap, ((0, 0), (0, LANES - experts)))
    vmem = pl.BlockSpec(memory_space=pltpu.VMEM)
    hbm = pl.BlockSpec(memory_space=pl.ANY)
    dma = pltpu.SemaphoreType.DMA
    both = pl.pallas_call(
        functools.partial(moe_kernel, nx, ny, ng, slots),
        out_shape=pltpu.VMEM((2 * tok, width), BF16),
        in_specs=[hbm] * 8,
        out_specs=vmem,
        scratch_shapes=[
            pltpu.VMEM((tok, width), BF16),
            pltpu.VMEM((tok, width), BF16),
            pltpu.VMEM((tok, top), BF16),
            pltpu.VMEM((tok, top), jnp.int32),
            pltpu.VMEM(cap.shape, jnp.int32),
            pltpu.VMEM((w, ff), BF16),
            pltpu.VMEM((w, ff), BF16),
            pltpu.VMEM((ff, w), BF16),
            pltpu.VMEM((8, LANES), F32),
            pltpu.VMEM((nl, 8, LANES), F32),
            pltpu.VMEM((nx, tok * ns, LANES), F32),
            pltpu.VMEM((nx, tok * ns, LANES), BF16),
            pltpu.VMEM((nl, tok * ns, LANES), BF16),
            pltpu.VMEM((nl * tok * ns, LANES), F32),
            pltpu.VMEM((group, rows), BF16),
            pltpu.VMEM((4, rows * nj, LANES), F32),
            pltpu.VMEM((2, ng, 2 * slots * nj, LANES), BF16),
            pltpu.VMEM((2, ng, 2 * slots * nj, LANES), BF16),
            pltpu.VMEM((2, rows, w), BF16),
            pltpu.VMEM((2, 2, 3, top_rows, fc), BF16),
            pltpu.VMEM((2, 2, 3, top_rows, fc), BF16),
        ] + [pltpu.VMEM((2, 2, 3, part_rows, fc), BF16)] * 6 + [
            pltpu.VMEM((2, nx, 3, part_rows, fc), BF16),
            pltpu.VMEM((2, rows, w), F32),
            pltpu.VMEM((nl * tok * ns, LANES), F32),
            pltpu.VMEM((nl, tok * ns, LANES), BF16),
            pltpu.VMEM((nl, tok * ns, LANES), BF16),
            dma((8,)),
            dma((2,)),
            dma((2,)),
            dma((2, 2, 2)),
            dma((4, 2, 2, 2)),
            dma((2, nx // 2, 2, 2)),
            dma((2, 2)),
            dma((2,)),
        ],
        compiler_params=pltpu.CompilerParams(
            collective_id=0, has_side_effects=True, vmem_limit_bytes=60 * 1024 * 1024),
    )(tokens, cotangent, gates, expert_ids, cap, w_gate, w_up, w_down)
    return both[:tok], both[tok:]


def solution(mesh):
    def run(tokens, cotangent, gates, expert_ids, capacity, w_gate, w_up, w_down):
        ng, local = mesh.shape["group"], mesh.shape["local"]
        w = w_gate.shape[0] // (ng * local)
        nx = tokens.shape[1] // w
        spec = P(("group", "local"), None)
        return jax.shard_map(
            functools.partial(per_device, nx, local // nx, ng),
            mesh=mesh,
            in_specs=(spec, spec, spec, spec, P(), spec, spec, P(None, ("group", "local"))),
            out_specs=(spec, spec),
            check_vma=False,
        )(tokens, cotangent, gates, expert_ids, capacity, w_gate, w_up, w_down)

    return run
```

```python
import functools

import jax
import jax.numpy as jnp
from jax import lax
from jax.experimental import pallas as pl
from jax.experimental.pallas import tpu as pltpu
from jax.sharding import PartitionSpec as P

LANES = 128
BF16 = jnp.bfloat16
F32 = jnp.float32
MESH = pl.DeviceIdType.MESH
CONTRACT_LAST = (((1,), (1,)), ((), ()))


def matmul(a, b):
    return jnp.dot(a, b, preferred_element_type=F32)


def matmul_t(a, b):
    return lax.dot_general(a, b, CONTRACT_LAST, preferred_element_type=F32)


def pieces(used):
    return -(-used // 16) * 16, used // 16 * 16


def moe_kernel(
    nx, ny, ng, slots,
    tokens_hbm, cotangent_hbm, gates_hbm, ids_hbm, cap_hbm, wg_hbm, wu_hbm, wd_hbm,
    result,
    tokens, cotangent, gates, ids, cap, wg, wu, wd,
    meta_out, meta_in, xs_f, xs, xr, xf, wsel_t, rows_f, zs, zr, acts,
    far_out, far_in, three_out, three_in, one_out, one_in, two_out, two_in, made, hid, acc, ho_f, ho, hi,
    load_sem, x_sem, m_sem, z_sem, rs_sem, ag_sem, sent_sem, h_sem,
):
    tok, width = tokens.shape
    top = ids.shape[1]
    w = wg.shape[0]
    fc = wg.shape[1] // nx
    nj = w // LANES
    ns = 2 * nj
    nl = nx * ny
    group = nl * tok
    rows = ng * slots
    part_rows = rows // 2
    top_rows = far_out.shape[3]
    used = slots * nj
    cuts = pieces(used)
    hx = nx // 2

    g = lax.axis_index("group")
    at = lax.axis_index("local")
    y = lax.div(at, nx)
    x = lax.rem(at, nx)

    def x_dev(k):
        return {"local": y * nx + lax.rem(x + k + nx, nx)}

    def each(low, high, body):
        def step(i, carry):
            body(i)
            return carry
        lax.fori_loop(low, high, step, 0)

    def far_first(p, n):
        return n // 2 + (p + 1) // 2 * (1 - 2 * (p % 2))

    x_order = [far_first(q, nx) for q in range(nx)]
    x_places = [lax.rem(x + k, nx) for k in x_order]

    def each_local(body, ahead=None):
        def line(p):
            there_y = lax.rem(y + ny // 2 + lax.div(p + 1, 2) * (1 - 2 * lax.rem(p, 2)), ny)
            if ahead is not None:
                ahead(there_y)
            for there in x_places:
                body(there_y * nx + there, there)

        each(0, ny - 1, line)
        if ahead is not None:
            ahead(y)
        for there in x_places[:-1]:
            body(y * nx + there, there)

    def each_group(body):
        each(0, ng - 1, lambda p: body(lax.rem(g + ng // 2 + lax.div(p + 1, 2) * (1 - 2 * lax.rem(p, 2)), ng)))

    def remote(src, dst, sems, index, device):
        return pltpu.make_async_remote_copy(
            src_ref=src, dst_ref=dst, send_sem=sems.at[(0,) + index], recv_sem=sems.at[(1,) + index],
            device_id=device, device_id_type=MESH)

    def all_of(ref, count, sems, index):
        part = ref.at[pl.ds(0, count)]
        return remote(part, part, sems, index, x_dev(1))

    loads = [pltpu.make_async_copy(a, b, load_sem.at[i]) for i, (a, b) in enumerate((
        (tokens_hbm, tokens), (cotangent_hbm, cotangent), (gates_hbm, gates), (ids_hbm, ids),
        (cap_hbm, cap), (wg_hbm, wg), (wu_hbm, wu), (wd_hbm, wd)))]
    small, weights = loads[:5], loads[5:]

    barrier = pltpu.get_barrier_semaphore()

    def greet(device):
        pl.semaphore_signal(barrier, inc=1, device_id=device, device_id_type=MESH)

    each_local(lambda there, tx: greet({"local": there}))
    each_group(lambda there: greet({"group": there}))
    for copy in loads:
        copy.start()

    with jax.named_scope("cut_tokens"):
        for copy in small:
            copy.wait()
        meta_out[...] = jnp.zeros_like(meta_out)
        meta_out[0:tok, 0:top] = ids[...].astype(F32)
        meta_out[0:tok, top:2 * top] = gates[...].astype(F32)

        def cut(dest):
            start = pl.multiple_of(dest * w, LANES)
            for side, ref in enumerate((tokens, cotangent)):
                v = ref[:, pl.ds(start, w)].astype(F32)
                for i in range(tok):
                    for j in range(nj):
                        r = i * ns + side * nj + j
                        xs_f[dest, r:r + 1, :] = v[i:i + 1, j * LANES:(j + 1) * LANES]

        each(0, nx, cut)
        xs[...] = xs_f[...].astype(BF16)
        xr[pl.ds(at, 1)] = xs[pl.ds(x, 1)]
        meta_in[pl.ds(at, 1)] = meta_out[...].reshape(1, 8, LANES)

    with jax.named_scope("entry_wait"):
        pl.semaphore_wait(barrier, nl + ng - 2)

    def send_meta(there, tx):
        remote(meta_out.at[pl.ds(0, tok)], meta_in.at[at, pl.ds(0, tok)], m_sem, (), {"local": there}).start()

    def send_block(there, tx):
        remote(xs.at[tx], xr.at[at], x_sem, (), {"local": there}).start()

    metas = all_of(meta_in.at[:, pl.ds(0, tok)], nl - 1, m_sem, ())
    blocks = all_of(xr, nl - 1, x_sem, ())

    with jax.named_scope("token_exchange"):
        each_local(send_meta)
        each_local(send_block)
        metas.wait_recv()

    with jax.named_scope("routing"):
        xf[0:nl * 8] = meta_in[...].reshape(nl * 8, LANES)
        meta = jnp.concatenate([xf[pl.ds(i, nl, stride=8), :] for i in range(tok)], 0)
        expert = lax.broadcasted_iota(jnp.int32, (group, LANES), 1).astype(F32)
        hit = jnp.zeros((group, LANES), F32)
        weight = jnp.zeros((group, LANES), F32)
        for k in range(top):
            same = meta[:, k:k + 1] == expert
            hit = jnp.where(same, 1.0, hit)
            weight = jnp.where(same, meta[:, top + k:top + k + 1], weight)

        def order(axis):
            p = lax.broadcasted_iota(jnp.int32, (group, group), axis)
            turn = jnp.where(p >= nl, 1, 0)
            for i in range(2, tok):
                turn = jnp.where(p >= i * nl, i, turn)
            return (p - turn * nl) * tok + turn

        earlier = order(1) < order(0)
        rank = matmul(jnp.where(earlier, 1.0, 0.0).astype(BF16), hit.astype(BF16))
        kept = (hit > 0.5) & (rank < cap[...].astype(F32))
        rank = jnp.where(kept, rank, -1.0).astype(BF16)
        weight = weight.astype(BF16)

        r_group = jnp.floor((lax.broadcasted_iota(jnp.int32, (rows, LANES), 0).astype(F32) + 0.5) * (1.0 / slots))
        r_expert = r_group * ny + y.astype(F32)
        pick = jnp.where(lax.broadcasted_iota(jnp.int32, (rows, LANES), 1).astype(F32) == r_expert, 1.0, 0.0).astype(BF16)
        r_at = lax.broadcasted_iota(jnp.int32, (rows, group), 0).astype(F32)
        r_slot = r_at - jnp.floor((r_at + 0.5) * (1.0 / slots)) * slots
        select = jnp.where(matmul_t(pick, rank) == r_slot, 1.0, 0.0).astype(BF16)
        c_at = lax.broadcasted_iota(jnp.int32, (group, rows), 1).astype(F32)
        c_slot = c_at - jnp.floor((c_at + 0.5) * (1.0 / slots)) * slots
        wsel_t[...] = jnp.where(matmul_t(rank, pick) == c_slot, matmul_t(weight, pick), 0.0).astype(BF16)

    def piece(way, index):
        low, high = (0, cuts[way]) if index == 0 else (cuts[way], 2 * used)
        return pl.ds(low, high - low)

    def row_blocks(way, index):
        return all_of(zr.at[way, :, piece(way, index)], ng - 1, z_sem, (way, index))

    def spread(way, index):
        low, high = (0, cuts[way]) if index == 0 else (cuts[way], 2 * used)
        here = piece(way, index)

        def part_of(dest):
            start = pl.multiple_of(dest * used, 8)
            parts = []
            if low < used:
                parts.append(rows_f[0, pl.ds(start + low, min(high, used) - low), :])
            if high > used:
                first = max(low, used)
                parts.append(rows_f[1, pl.ds(start + first - used, high - first), :])
            return jnp.concatenate(parts, 0).astype(BF16)

        def go(dest):
            zs[way, dest, here] = part_of(dest)
            remote(zs.at[way, dest, here], zr.at[way, g, here], z_sem, (way, index), {"group": dest}).start()

        each_group(go)
        zr[way, g, here] = part_of(g)

    def lay_out(side, got):
        rows_f[2 + side] = got.astype(F32).reshape(ng * used, LANES)
        return [rows_f[2 + side, pl.ds(j, rows, stride=nj), :].astype(BF16) for j in range(nj)]

    with jax.named_scope("token_wait"):
        blocks.wait_recv()

    with jax.named_scope("row_send"):
        xf[...] = xr[...].astype(F32).reshape(nl * tok * ns, LANES)
        for side in range(2):
            for j in range(nj):
                held = jnp.concatenate(
                    [xf[pl.ds(i * ns + side * nj + j, nl, stride=tok * ns), :] for i in range(tok)], 0).astype(BF16)
                rows_f[side, pl.ds(j, rows, stride=nj), :] = matmul(select, held)
        spread(0, 0)
        spread(0, 1)

    def lanes_of(chunk):
        return pl.ds(pl.multiple_of(chunk * fc, LANES), fc)

    def of(part):
        return pl.ds(part * part_rows, part_rows)

    def chunk_at(k):
        return lax.rem(x + k + nx, nx)

    def products(kind, k):
        here = lanes_of(chunk_at(k))
        if kind == 0:
            both = matmul(acts[0], jnp.concatenate([wg[:, here], wu[:, here]], 1))
            return [(0, both[:, 0:fc]), (1, both[:, fc:2 * fc])]
        return [(2, matmul_t(acts[1], wd[here, :]))]

    near = (2, -2, 1, -1, 0)

    def products_ahead(kind):
        for index, k in enumerate(near):
            for m, value in products(kind, k):
                made[index, m] = value

    def ready(kind, part, k):
        return [(m, made[near.index(k), m, of(part)]) for m in ((0, 1), (2,))[kind]]

    FAR, THREE, TWO, ONE = range(4)
    routes = {FAR: (far_out, far_in, 2), THREE: (three_out, three_in, 1), TWO: (two_out, two_in, 1),
              ONE: (one_out, one_in, 1)}
    signs = (1, -1)
    rs_kinds = (pl.ds(0, 2), pl.ds(2, 1))
    ag_kinds = (pl.ds(0, 1), pl.ds(1, 2))

    def far_span(part, way):
        cut = top_rows if part == 0 else part_rows - top_rows
        return (0, cut) if way == 0 else (cut, part_rows)

    def one_way(src, dst, send_sem, recv_sem, device):
        return pltpu.make_async_remote_copy(
            src_ref=src, dst_ref=dst, send_sem=send_sem, recv_sem=recv_sem, device_id=device, device_id_type=MESH)

    def rs_copy(route, way, kind, part):
        out, into, distance = routes[route]
        out, into = out.at[part, way, rs_kinds[kind]], into.at[part, way, rs_kinds[kind]]
        if route == FAR:
            low, high = far_span(part, way)
            out, into = out.at[:, pl.ds(0, high - low)], into.at[:, pl.ds(0, high - low)]
        return one_way(out, into, sent_sem.at[0, part], rs_sem.at[route, way, kind, part], x_dev(signs[way] * distance))

    def rs_start(kind):
        shared = products(kind, hx)
        for part in range(2):
            first = part * part_rows
            for way in range(2):
                low, high = far_span(part, way)
                for m, value in shared:
                    far_out[part, way, m, 0:high - low] = value[first + low:first + high].astype(BF16)
                rs_copy(FAR, way, kind, part).start()
        threes = []
        for way in range(2):
            threes.append(products(kind, signs[way] * 3))
        for part in range(2):
            for way in range(2):
                for m, value in threes[way]:
                    three_out[part, way, m] = value[part * part_rows:(part + 1) * part_rows].astype(BF16)
                rs_copy(THREE, way, kind, part).start()

    def rs_two(kind, part):
        for way in range(2):
            mine = ready(kind, part, signs[way] * 2)
            rs_copy(FAR, way, kind, part).wait_recv()
            rs_copy(THREE, way, kind, part).wait_recv()
            low, high = far_span(part, way)
            for m, value in mine:
                value = value + three_in[part, way, m].astype(F32)
                add = value[low:high] + far_in[part, way, m, 0:high - low].astype(F32)
                two_out[part, way, m, low:high] = add.astype(BF16)
                if way == 0:
                    two_out[part, way, m, high:part_rows] = value[high:part_rows].astype(BF16)
                else:
                    two_out[part, way, m, 0:low] = value[0:low].astype(BF16)
            rs_copy(TWO, way, kind, part).start()

    def rs_one(kind, part):
        for way in range(2):
            mine = ready(kind, part, signs[way])
            rs_copy(TWO, way, kind, part).wait_recv()
            for m, value in mine:
                one_out[part, way, m] = (value + two_in[part, way, m].astype(F32)).astype(BF16)
            rs_copy(ONE, way, kind, part).start()

    def rs_last(kind, part):
        mine = ready(kind, part, 0)
        for way in range(2):
            rs_copy(ONE, way, kind, part).wait_recv()
        return [value + (one_in[part, 0, m].astype(F32) + one_in[part, 1, m].astype(F32)) for m, value in mine]

    def ag_copy(way, distance, kind, part, receive=False):
        back = distance if receive else min(distance - 1, 2)
        ref = hid.at[part, chunk_at(-signs[way] * back), ag_kinds[kind]]
        if distance == hx:
            low, high = far_span(part, way)
            ref = ref.at[:, pl.ds(low, high - low)]
        hop = distance - min(distance - 1, 2)
        return one_way(ref, ref, sent_sem.at[1, part], ag_sem.at[way, distance - 1, kind, part], x_dev(signs[way] * hop))

    def ag_start(kind, part):
        for way in range(2):
            ag_copy(way, 1, kind, part).start()

    def ag_pass(kind, part, distance):
        for way in range(2):
            ag_copy(way, distance, kind, part, True).wait_recv()
            for further in (2,) if distance == 1 else range(hx, 2, -1):
                ag_copy(way, further, kind, part).start()

    def ag_wait(kind, part, distance):
        for way in range(2):
            ag_copy(way, distance, kind, part, True).wait_recv()

    def add_out(part, k):
        chunk = chunk_at(k)
        acc[0, of(part)] += matmul(hid[part, chunk, 0], wd[lanes_of(chunk), :])

    def add_grad(part, k):
        chunk = chunk_at(k)
        here = lanes_of(chunk)
        acc[1, of(part)] += matmul_t(jnp.concatenate([hid[part, chunk, 1], hid[part, chunk, 2]], 1),
                                     jnp.concatenate([wg[:, here], wu[:, here]], 1))

    adds = (add_out, add_grad)

    def add_both(kind, part, distance):
        adds[kind](part, distance)
        adds[kind](part, -distance)

    def add_rest(kind):
        for distance in range(3, hx):
            for part in range(2):
                ag_wait(kind, part, distance)
                add_both(kind, part, distance)
        for part in range(2):
            ag_wait(kind, part, hx)
            adds[kind](part, hx)

    with jax.named_scope("rows_wait"):
        row_blocks(0, 0).wait_recv()
        for j, part in enumerate(lay_out(0, zr[0, :, 0:cuts[0]].astype(F32)[:, 0:used])):
            acts[0, :, j * LANES:(j + 1) * LANES] = part
        for copy in weights:
            copy.wait()

    with jax.named_scope("gate_up_start"):
        rs_start(0)

    with jax.named_scope("cotangent_wait"):
        row_blocks(0, 1).wait_recv()
        for j, part in enumerate(lay_out(1, zr[0].astype(F32)[:, used:2 * used])):
            acts[1, :, j * LANES:(j + 1) * LANES] = part

    with jax.named_scope("back_start"):
        rs_start(1)

    with jax.named_scope("products_ahead"):
        products_ahead(0)

    with jax.named_scope("gate_up_two"):
        rs_two(0, 0)
        products_ahead(1)
        acc[...] = jnp.zeros_like(acc)
        rs_two(0, 1)

    with jax.named_scope("back_two"):
        for part in range(2):
            rs_two(1, part)

    with jax.named_scope("gate_up_one"):
        for part in range(2):
            rs_one(0, part)

    with jax.named_scope("back_one"):
        for part in range(2):
            rs_one(1, part)

    with jax.named_scope("gate_up_last"):
        saved = []
        for part in range(2):
            gate_pre, up_pre = rs_last(0, part)
            sig = jax.nn.sigmoid(gate_pre)
            silu = gate_pre * sig
            hid[part, x, 0] = (silu * up_pre).astype(BF16)
            ag_start(0, part)
            saved.append((up_pre * sig * (1.0 + gate_pre * (1.0 - sig)), silu))

    with jax.named_scope("back_last"):
        for part in range(2):
            (d_hidden,) = rs_last(1, part)
            hid[part, x, 1] = (d_hidden * saved[part][0]).astype(BF16)
            hid[part, x, 2] = (d_hidden * saved[part][1]).astype(BF16)
            ag_start(1, part)

    with jax.named_scope("hidden_pass_one"):
        for part in range(2):
            add_out(part, 0)
            ag_pass(0, part, 1)

    with jax.named_scope("grad_pass_one"):
        for part in range(2):
            add_grad(part, 0)
            ag_pass(1, part, 1)

    with jax.named_scope("hidden_pass_two"):
        for part in range(2):
            add_both(0, part, 1)
            ag_pass(0, part, 2)

    with jax.named_scope("grad_pass_two"):
        for part in range(2):
            add_both(1, part, 1)
            ag_pass(1, part, 2)

    with jax.named_scope("out_rest"):
        for part in range(2):
            add_both(0, part, 2)
        add_rest(0)

    def send_back(side):
        for j in range(nj):
            rows_f[side, pl.ds(j, rows, stride=nj), :] = acc[side, :, j * LANES:(j + 1) * LANES]
        spread(1, side)

    with jax.named_scope("out_send"):
        send_back(0)

    with jax.named_scope("grad_rest"):
        for part in range(2):
            add_both(1, part, 2)
        add_rest(1)

    with jax.named_scope("grad_send"):
        send_back(1)

    mine = tok * ns
    sums = all_of(hi, nl - 1, h_sem, ())

    def weigh(side):
        for j, part in enumerate(lay_out(side, zr[1].astype(F32)[:, side * used:(side + 1) * used])):
            total = matmul(wsel_t[...], part)
            for i in range(tok):
                ho_f[pl.ds((side * tok + i) * nj + j, nl, stride=mine), :] = total[i * nl:(i + 1) * nl]

    def send_home(there, tx):
        remote(ho.at[there], hi.at[at], h_sem, (), {"local": there}).start()

    def round_line(line):
        size = nx * mine
        start = pl.multiple_of(line * size, size)
        ho[pl.ds(line * nx, nx)] = ho_f[pl.ds(start, size), :].astype(BF16).reshape(nx, mine, LANES)

    with jax.named_scope("back_wait"):
        for index in range(2):
            row_blocks(1, index).wait_recv()

    with jax.named_scope("grad_rows"):
        for side in range(2):
            weigh(side)

    with jax.named_scope("home_send"):
        each_local(send_home, round_line)
        hi[pl.ds(at, 1)] = ho[pl.ds(at, 1)]

    with jax.named_scope("home_wait"):
        sums.wait_recv()

    with jax.named_scope("finish"):
        total = jnp.sum(hi[...].astype(F32).reshape(ny, nx, mine, LANES), axis=0)
        whole = []
        for src in range(nx):
            for j in range(nj):
                whole.append(jnp.concatenate([total[src, i * nj + j:i * nj + j + 1] for i in range(2 * tok)], 0))
        result[...] = jnp.concatenate(whole, 1).astype(BF16)

    with jax.named_scope("drain"):
        metas.wait_send()
        blocks.wait_send()
        sums.wait_send()
        for index in range(2):
            for way in range(2):
                row_blocks(way, index).wait_send()
        for stage in range(2):
            for part in range(2):
                chunks = hid.at[part, pl.ds(0, nx - 1)]
                one_way(chunks, chunks, sent_sem.at[stage, part], rs_sem.at[0, 0, 0, 0], x_dev(1)).wait_send()


def per_device(nx, ny, ng, tokens, cotangent, gates, expert_ids, capacity, w_gate, w_up, w_down):
    tok, width = tokens.shape
    top = expert_ids.shape[1]
    w, ff = w_gate.shape
    experts = capacity.shape[0]
    nl = nx * ny
    group = nl * tok
    slots = min(group * top // experts * 5 // 4, group)
    rows = ng * slots
    nj = w // LANES
    ns = 2 * nj
    fc = ff // nx
    part_rows = rows // 2
    top_rows = -(-part_rows // 32) * 16
    if top_rows >= part_rows:
        top_rows = part_rows // 2
    cap = capacity.reshape(1, experts)
    if experts < LANES:
        cap = jnp.pad(cap, ((0, 0), (0, LANES - experts)))
    vmem = pl.BlockSpec(memory_space=pltpu.VMEM)
    hbm = pl.BlockSpec(memory_space=pl.ANY)
    dma = pltpu.SemaphoreType.DMA
    both = pl.pallas_call(
        functools.partial(moe_kernel, nx, ny, ng, slots),
        out_shape=pltpu.VMEM((2 * tok, width), BF16),
        in_specs=[hbm] * 8,
        out_specs=vmem,
        scratch_shapes=[
            pltpu.VMEM((tok, width), BF16),
            pltpu.VMEM((tok, width), BF16),
            pltpu.VMEM((tok, top), BF16),
            pltpu.VMEM((tok, top), jnp.int32),
            pltpu.VMEM(cap.shape, jnp.int32),
            pltpu.VMEM((w, ff), BF16),
            pltpu.VMEM((w, ff), BF16),
            pltpu.VMEM((ff, w), BF16),
            pltpu.VMEM((8, LANES), F32),
            pltpu.VMEM((nl, 8, LANES), F32),
            pltpu.VMEM((nx, tok * ns, LANES), F32),
            pltpu.VMEM((nx, tok * ns, LANES), BF16),
            pltpu.VMEM((nl, tok * ns, LANES), BF16),
            pltpu.VMEM((nl * tok * ns, LANES), F32),
            pltpu.VMEM((group, rows), BF16),
            pltpu.VMEM((4, rows * nj, LANES), F32),
            pltpu.VMEM((2, ng, 2 * slots * nj, LANES), BF16),
            pltpu.VMEM((2, ng, 2 * slots * nj, LANES), BF16),
            pltpu.VMEM((2, rows, w), BF16),
            pltpu.VMEM((2, 2, 3, top_rows, fc), BF16),
            pltpu.VMEM((2, 2, 3, top_rows, fc), BF16),
        ] + [pltpu.VMEM((2, 2, 3, part_rows, fc), BF16)] * 6 + [
            pltpu.VMEM((5, 3, rows, fc), F32),
            pltpu.VMEM((2, nx, 3, part_rows, fc), BF16),
            pltpu.VMEM((2, rows, w), F32),
            pltpu.VMEM((nl * tok * ns, LANES), F32),
            pltpu.VMEM((nl, tok * ns, LANES), BF16),
            pltpu.VMEM((nl, tok * ns, LANES), BF16),
            dma((8,)),
            dma((2,)),
            dma((2,)),
            dma((2, 2, 2)),
            dma((4, 2, 2, 2)),
            dma((2, nx // 2, 2, 2)),
            dma((2, 2)),
            dma((2,)),
        ],
        compiler_params=pltpu.CompilerParams(
            collective_id=0, has_side_effects=True, vmem_limit_bytes=60 * 1024 * 1024),
    )(tokens, cotangent, gates, expert_ids, cap, w_gate, w_up, w_down)
    return both[:tok], both[tok:]


def solution(mesh):
    def run(tokens, cotangent, gates, expert_ids, capacity, w_gate, w_up, w_down):
        ng, local = mesh.shape["group"], mesh.shape["local"]
        w = w_gate.shape[0] // (ng * local)
        nx = tokens.shape[1] // w
        spec = P(("group", "local"), None)
        return jax.shard_map(
            functools.partial(per_device, nx, local // nx, ng),
            mesh=mesh,
            in_specs=(spec, spec, spec, spec, P(), spec, spec, P(None, ("group", "local"))),
            out_specs=(spec, spec),
            check_vma=False,
        )(tokens, cotangent, gates, expert_ids, capacity, w_gate, w_up, w_down)

    return run
```

```python
import functools

import jax
import jax.numpy as jnp
from jax import lax
from jax.experimental import pallas as pl
from jax.experimental.pallas import tpu as pltpu
from jax.sharding import PartitionSpec as P

LANES = 128
BF16 = jnp.bfloat16
F32 = jnp.float32
MESH = pl.DeviceIdType.MESH
CONTRACT_LAST = (((1,), (1,)), ((), ()))


def matmul(a, b):
    return jnp.dot(a, b, preferred_element_type=F32)


def matmul_t(a, b):
    return lax.dot_general(a, b, CONTRACT_LAST, preferred_element_type=F32)


def pieces(used):
    return -(-used // 16) * 16, used // 16 * 16


def moe_kernel(
    nx, ny, ng, slots,
    tokens_hbm, cotangent_hbm, gates_hbm, ids_hbm, cap_hbm, wg_hbm, wu_hbm, wd_hbm,
    result,
    tokens, cotangent, gates, ids, cap, wg, wu, wd,
    meta_out, meta_in, xs_f, xs, xr, xf, wsel_t, rows_f, zs, zr, acts,
    far_out, far_in, three_out, three_in, one_out, one_in, two_out, two_in, made, hid, acc, ho_f, ho, hi,
    load_sem, x_sem, m_sem, z_sem, rs_sem, ag_sem, sent_sem, h_sem,
):
    tok, width = tokens.shape
    top = ids.shape[1]
    w = wg.shape[0]
    fc = wg.shape[1] // nx
    nj = w // LANES
    ns = 2 * nj
    nl = nx * ny
    group = nl * tok
    rows = ng * slots
    part_rows = rows // 2
    top_rows = far_out.shape[3]
    used = slots * nj
    cuts = pieces(used)
    hx = nx // 2

    g = lax.axis_index("group")
    at = lax.axis_index("local")
    y = lax.div(at, nx)
    x = lax.rem(at, nx)

    def x_dev(k):
        return {"local": y * nx + lax.rem(x + k + nx, nx)}

    def each(low, high, body):
        def step(i, carry):
            body(i)
            return carry
        lax.fori_loop(low, high, step, 0)

    def far_first(p, n):
        return n // 2 + (p + 1) // 2 * (1 - 2 * (p % 2))

    x_order = [far_first(q, nx) for q in range(nx)]
    x_places = [lax.rem(x + k, nx) for k in x_order]

    def each_local(body, ahead=None):
        def line(p):
            there_y = lax.rem(y + ny // 2 + lax.div(p + 1, 2) * (1 - 2 * lax.rem(p, 2)), ny)
            if ahead is not None:
                ahead(there_y)
            for there in x_places:
                body(there_y * nx + there, there)

        each(0, ny - 1, line)
        if ahead is not None:
            ahead(y)
        for there in x_places[:-1]:
            body(y * nx + there, there)

    def each_group(body):
        each(0, ng - 1, lambda p: body(lax.rem(g + ng // 2 + lax.div(p + 1, 2) * (1 - 2 * lax.rem(p, 2)), ng)))

    def remote(src, dst, sems, index, device):
        return pltpu.make_async_remote_copy(
            src_ref=src, dst_ref=dst, send_sem=sems.at[(0,) + index], recv_sem=sems.at[(1,) + index],
            device_id=device, device_id_type=MESH)

    def all_of(ref, count, sems, index):
        part = ref.at[pl.ds(0, count)]
        return remote(part, part, sems, index, x_dev(1))

    loads = [pltpu.make_async_copy(a, b, load_sem.at[i]) for i, (a, b) in enumerate((
        (tokens_hbm, tokens), (cotangent_hbm, cotangent), (gates_hbm, gates), (ids_hbm, ids),
        (cap_hbm, cap), (wg_hbm, wg), (wu_hbm, wu), (wd_hbm, wd)))]
    small, weights = loads[:5], loads[5:]

    barrier = pltpu.get_barrier_semaphore()

    def greet(device):
        pl.semaphore_signal(barrier, inc=1, device_id=device, device_id_type=MESH)

    each_local(lambda there, tx: greet({"local": there}))
    each_group(lambda there: greet({"group": there}))
    for copy in loads:
        copy.start()

    with jax.named_scope("cut_tokens"):
        for copy in small:
            copy.wait()
        meta_out[...] = jnp.zeros_like(meta_out)
        meta_out[0:tok, 0:top] = ids[...].astype(F32)
        meta_out[0:tok, top:2 * top] = gates[...].astype(F32)

        def cut(dest):
            start = pl.multiple_of(dest * w, LANES)
            for side, ref in enumerate((tokens, cotangent)):
                v = ref[:, pl.ds(start, w)].astype(F32)
                for i in range(tok):
                    for j in range(nj):
                        r = i * ns + side * nj + j
                        xs_f[dest, r:r + 1, :] = v[i:i + 1, j * LANES:(j + 1) * LANES]

        each(0, nx, cut)
        xs[...] = xs_f[...].astype(BF16)
        xr[pl.ds(at, 1)] = xs[pl.ds(x, 1)]
        meta_in[pl.ds(at, 1)] = meta_out[...].reshape(1, 8, LANES)

    with jax.named_scope("entry_wait"):
        pl.semaphore_wait(barrier, nl + ng - 2)

    def send_meta(there, tx):
        remote(meta_out.at[pl.ds(0, tok)], meta_in.at[at, pl.ds(0, tok)], m_sem, (), {"local": there}).start()

    def send_block(there, tx):
        remote(xs.at[tx], xr.at[at], x_sem, (), {"local": there}).start()

    metas = all_of(meta_in.at[:, pl.ds(0, tok)], nl - 1, m_sem, ())
    blocks = all_of(xr, nl - 1, x_sem, ())

    with jax.named_scope("token_exchange"):
        each_local(send_meta)
        each_local(send_block)
        metas.wait_recv()

    with jax.named_scope("routing"):
        xf[0:nl * 8] = meta_in[...].reshape(nl * 8, LANES)
        meta = jnp.concatenate([xf[pl.ds(i, nl, stride=8), :] for i in range(tok)], 0)
        expert = lax.broadcasted_iota(jnp.int32, (group, LANES), 1).astype(F32)
        hit = jnp.zeros((group, LANES), F32)
        weight = jnp.zeros((group, LANES), F32)
        for k in range(top):
            same = meta[:, k:k + 1] == expert
            hit = jnp.where(same, 1.0, hit)
            weight = jnp.where(same, meta[:, top + k:top + k + 1], weight)

        def order(axis):
            p = lax.broadcasted_iota(jnp.int32, (group, group), axis)
            turn = jnp.where(p >= nl, 1, 0)
            for i in range(2, tok):
                turn = jnp.where(p >= i * nl, i, turn)
            return (p - turn * nl) * tok + turn

        earlier = order(1) < order(0)
        rank = matmul(jnp.where(earlier, 1.0, 0.0).astype(BF16), hit.astype(BF16))
        kept = (hit > 0.5) & (rank < cap[...].astype(F32))
        rank = jnp.where(kept, rank, -1.0).astype(BF16)
        weight = weight.astype(BF16)

        r_group = jnp.floor((lax.broadcasted_iota(jnp.int32, (rows, LANES), 0).astype(F32) + 0.5) * (1.0 / slots))
        r_expert = r_group * ny + y.astype(F32)
        pick = jnp.where(lax.broadcasted_iota(jnp.int32, (rows, LANES), 1).astype(F32) == r_expert, 1.0, 0.0).astype(BF16)
        r_at = lax.broadcasted_iota(jnp.int32, (rows, group), 0).astype(F32)
        r_slot = r_at - jnp.floor((r_at + 0.5) * (1.0 / slots)) * slots
        select = jnp.where(matmul_t(pick, rank) == r_slot, 1.0, 0.0).astype(BF16)
        c_at = lax.broadcasted_iota(jnp.int32, (group, rows), 1).astype(F32)
        c_slot = c_at - jnp.floor((c_at + 0.5) * (1.0 / slots)) * slots
        wsel_t[...] = jnp.where(matmul_t(rank, pick) == c_slot, matmul_t(weight, pick), 0.0).astype(BF16)

    def piece(way, index):
        low, high = (0, cuts[way]) if index == 0 else (cuts[way], 2 * used)
        return pl.ds(low, high - low)

    def row_blocks(way, index):
        return all_of(zr.at[way, :, piece(way, index)], ng - 1, z_sem, (way, index))

    def spread(way, index):
        low, high = (0, cuts[way]) if index == 0 else (cuts[way], 2 * used)
        here = piece(way, index)

        def part_of(dest):
            start = pl.multiple_of(dest * used, 8)
            parts = []
            if low < used:
                parts.append(rows_f[0, pl.ds(start + low, min(high, used) - low), :])
            if high > used:
                first = max(low, used)
                parts.append(rows_f[1, pl.ds(start + first - used, high - first), :])
            return jnp.concatenate(parts, 0).astype(BF16)

        def go(dest):
            zs[way, dest, here] = part_of(dest)
            remote(zs.at[way, dest, here], zr.at[way, g, here], z_sem, (way, index), {"group": dest}).start()

        each_group(go)
        zr[way, g, here] = part_of(g)

    def lay_out(side, got):
        rows_f[2 + side] = got.astype(F32).reshape(ng * used, LANES)
        return [rows_f[2 + side, pl.ds(j, rows, stride=nj), :].astype(BF16) for j in range(nj)]

    with jax.named_scope("token_wait"):
        blocks.wait_recv()

    with jax.named_scope("row_send"):
        xf[...] = xr[...].astype(F32).reshape(nl * tok * ns, LANES)
        for side in range(2):
            for j in range(nj):
                held = jnp.concatenate(
                    [xf[pl.ds(i * ns + side * nj + j, nl, stride=tok * ns), :] for i in range(tok)], 0).astype(BF16)
                rows_f[side, pl.ds(j, rows, stride=nj), :] = matmul(select, held)
        spread(0, 0)
        spread(0, 1)

    def lanes_of(chunk):
        return pl.ds(pl.multiple_of(chunk * fc, LANES), fc)

    def of(part):
        return pl.ds(part * part_rows, part_rows)

    def chunk_at(k):
        return lax.rem(x + k + nx, nx)

    def products(kind, here_rows, k):
        here = lanes_of(chunk_at(k))
        if kind == 0:
            both = matmul(acts[0, here_rows], jnp.concatenate([wg[:, here], wu[:, here]], 1))
            return [(0, both[:, 0:fc]), (1, both[:, fc:2 * fc])]
        return [(2, matmul_t(acts[1, here_rows], wd[here, :]))]

    near = (2, -2, 1, -1, 0)

    def products_ahead(kind):
        for index, k in enumerate(near):
            for m, value in products(kind, pl.ds(0, rows), k):
                made[index, m] = value

    def ready(kind, part, k):
        return [(m, made[near.index(k), m, of(part)]) for m in ((0, 1), (2,))[kind]]

    FAR, THREE, TWO, ONE = range(4)
    routes = {FAR: (far_out, far_in, 2), THREE: (three_out, three_in, 1), TWO: (two_out, two_in, 1),
              ONE: (one_out, one_in, 1)}
    signs = (1, -1)
    rs_kinds = (pl.ds(0, 2), pl.ds(2, 1))
    ag_kinds = (pl.ds(0, 1), pl.ds(1, 2))

    def far_span(part, way):
        cut = top_rows if part == 0 else part_rows - top_rows
        return (0, cut) if way == 0 else (cut, part_rows)

    def one_way(src, dst, send_sem, recv_sem, device):
        return pltpu.make_async_remote_copy(
            src_ref=src, dst_ref=dst, send_sem=send_sem, recv_sem=recv_sem, device_id=device, device_id_type=MESH)

    def rs_copy(route, way, kind, part):
        out, into, distance = routes[route]
        out, into = out.at[part, way, rs_kinds[kind]], into.at[part, way, rs_kinds[kind]]
        if route == FAR:
            low, high = far_span(part, way)
            out, into = out.at[:, pl.ds(0, high - low)], into.at[:, pl.ds(0, high - low)]
        return one_way(out, into, sent_sem.at[0, part], rs_sem.at[route, way, kind, part], x_dev(signs[way] * distance))

    def rs_start(kind, part):
        shared = products(kind, of(part), hx)
        for way in range(2):
            low, high = far_span(part, way)
            for m, value in shared:
                far_out[part, way, m, 0:high - low] = value[low:high].astype(BF16)
            rs_copy(FAR, way, kind, part).start()
        for way in range(2):
            for m, value in products(kind, of(part), signs[way] * 3):
                three_out[part, way, m] = value.astype(BF16)
            rs_copy(THREE, way, kind, part).start()

    def rs_two(kind, part):
        for way in range(2):
            mine = ready(kind, part, signs[way] * 2)
            rs_copy(FAR, way, kind, part).wait_recv()
            rs_copy(THREE, way, kind, part).wait_recv()
            low, high = far_span(part, way)
            for m, value in mine:
                value = value + three_in[part, way, m].astype(F32)
                add = value[low:high] + far_in[part, way, m, 0:high - low].astype(F32)
                two_out[part, way, m, low:high] = add.astype(BF16)
                if way == 0:
                    two_out[part, way, m, high:part_rows] = value[high:part_rows].astype(BF16)
                else:
                    two_out[part, way, m, 0:low] = value[0:low].astype(BF16)
            rs_copy(TWO, way, kind, part).start()

    def rs_one(kind, part):
        for way in range(2):
            mine = ready(kind, part, signs[way])
            rs_copy(TWO, way, kind, part).wait_recv()
            for m, value in mine:
                one_out[part, way, m] = (value + two_in[part, way, m].astype(F32)).astype(BF16)
            rs_copy(ONE, way, kind, part).start()

    def rs_last(kind, part):
        mine = ready(kind, part, 0)
        for way in range(2):
            rs_copy(ONE, way, kind, part).wait_recv()
        return [value + (one_in[part, 0, m].astype(F32) + one_in[part, 1, m].astype(F32)) for m, value in mine]

    def ag_copy(way, distance, kind, part, receive=False):
        back = distance if receive else min(distance - 1, 2)
        ref = hid.at[part, chunk_at(-signs[way] * back), ag_kinds[kind]]
        if distance == hx:
            low, high = far_span(part, way)
            ref = ref.at[:, pl.ds(low, high - low)]
        hop = distance - min(distance - 1, 2)
        return one_way(ref, ref, sent_sem.at[1, part], ag_sem.at[way, distance - 1, kind, part], x_dev(signs[way] * hop))

    def ag_start(kind, part):
        for way in range(2):
            ag_copy(way, 1, kind, part).start()

    def ag_pass(kind, part, distance):
        for way in range(2):
            ag_copy(way, distance, kind, part, True).wait_recv()
            for further in (2,) if distance == 1 else range(hx, 2, -1):
                ag_copy(way, further, kind, part).start()

    def ag_wait(kind, part, distance):
        for way in range(2):
            ag_copy(way, distance, kind, part, True).wait_recv()

    def add_out(part, k):
        chunk = chunk_at(k)
        acc[0, of(part)] += matmul(hid[part, chunk, 0], wd[lanes_of(chunk), :])

    def add_grad(part, k):
        chunk = chunk_at(k)
        here = lanes_of(chunk)
        acc[1, of(part)] += matmul_t(jnp.concatenate([hid[part, chunk, 1], hid[part, chunk, 2]], 1),
                                     jnp.concatenate([wg[:, here], wu[:, here]], 1))

    adds = (add_out, add_grad)

    def add_both(kind, part, distance):
        adds[kind](part, distance)
        adds[kind](part, -distance)

    def add_rest(kind):
        for distance in range(3, hx):
            for part in range(2):
                ag_wait(kind, part, distance)
                add_both(kind, part, distance)
        for part in range(2):
            ag_wait(kind, part, hx)
            adds[kind](part, hx)

    with jax.named_scope("rows_wait"):
        row_blocks(0, 0).wait_recv()
        for j, part in enumerate(lay_out(0, zr[0, :, 0:cuts[0]].astype(F32)[:, 0:used])):
            acts[0, :, j * LANES:(j + 1) * LANES] = part
        for copy in weights:
            copy.wait()

    with jax.named_scope("gate_up_start"):
        for part in range(2):
            rs_start(0, part)

    with jax.named_scope("cotangent_wait"):
        row_blocks(0, 1).wait_recv()
        for j, part in enumerate(lay_out(1, zr[0].astype(F32)[:, used:2 * used])):
            acts[1, :, j * LANES:(j + 1) * LANES] = part

    with jax.named_scope("back_start"):
        for part in range(2):
            rs_start(1, part)

    with jax.named_scope("products_ahead"):
        products_ahead(0)

    with jax.named_scope("gate_up_two"):
        rs_two(0, 0)
        products_ahead(1)
        acc[...] = jnp.zeros_like(acc)
        rs_two(0, 1)

    with jax.named_scope("back_two"):
        for part in range(2):
            rs_two(1, part)

    with jax.named_scope("gate_up_one"):
        for part in range(2):
            rs_one(0, part)

    with jax.named_scope("back_one"):
        for part in range(2):
            rs_one(1, part)

    with jax.named_scope("gate_up_last"):
        saved = []
        for part in range(2):
            gate_pre, up_pre = rs_last(0, part)
            sig = jax.nn.sigmoid(gate_pre)
            silu = gate_pre * sig
            hid[part, x, 0] = (silu * up_pre).astype(BF16)
            ag_start(0, part)
            saved.append((up_pre * sig * (1.0 + gate_pre * (1.0 - sig)), silu))

    with jax.named_scope("back_last"):
        for part in range(2):
            (d_hidden,) = rs_last(1, part)
            hid[part, x, 1] = (d_hidden * saved[part][0]).astype(BF16)
            hid[part, x, 2] = (d_hidden * saved[part][1]).astype(BF16)
            ag_start(1, part)

    with jax.named_scope("hidden_pass_one"):
        for part in range(2):
            add_out(part, 0)
            ag_pass(0, part, 1)

    with jax.named_scope("grad_pass_one"):
        for part in range(2):
            add_grad(part, 0)
            ag_pass(1, part, 1)

    with jax.named_scope("hidden_pass_two"):
        for part in range(2):
            add_both(0, part, 1)
            ag_pass(0, part, 2)

    with jax.named_scope("grad_pass_two"):
        for part in range(2):
            add_both(1, part, 1)
            ag_pass(1, part, 2)

    with jax.named_scope("out_rest"):
        for part in range(2):
            add_both(0, part, 2)
        add_rest(0)

    def send_back(side):
        for j in range(nj):
            rows_f[side, pl.ds(j, rows, stride=nj), :] = acc[side, :, j * LANES:(j + 1) * LANES]
        spread(1, side)

    with jax.named_scope("out_send"):
        send_back(0)

    with jax.named_scope("grad_rest"):
        for part in range(2):
            add_both(1, part, 2)
        add_rest(1)

    with jax.named_scope("grad_send"):
        send_back(1)

    mine = tok * ns
    sums = all_of(hi, nl - 1, h_sem, ())

    def weigh(side):
        for j, part in enumerate(lay_out(side, zr[1].astype(F32)[:, side * used:(side + 1) * used])):
            total = matmul(wsel_t[...], part)
            for i in range(tok):
                ho_f[pl.ds((side * tok + i) * nj + j, nl, stride=mine), :] = total[i * nl:(i + 1) * nl]

    def send_home(there, tx):
        remote(ho.at[there], hi.at[at], h_sem, (), {"local": there}).start()

    def round_line(line):
        size = nx * mine
        start = pl.multiple_of(line * size, size)
        ho[pl.ds(line * nx, nx)] = ho_f[pl.ds(start, size), :].astype(BF16).reshape(nx, mine, LANES)

    with jax.named_scope("back_wait"):
        for index in range(2):
            row_blocks(1, index).wait_recv()

    with jax.named_scope("grad_rows"):
        for side in range(2):
            weigh(side)

    with jax.named_scope("home_send"):
        each_local(send_home, round_line)
        hi[pl.ds(at, 1)] = ho[pl.ds(at, 1)]

    with jax.named_scope("home_wait"):
        sums.wait_recv()

    with jax.named_scope("finish"):
        total = jnp.sum(hi[...].astype(F32).reshape(ny, nx, mine, LANES), axis=0)
        whole = []
        for src in range(nx):
            for j in range(nj):
                whole.append(jnp.concatenate([total[src, i * nj + j:i * nj + j + 1] for i in range(2 * tok)], 0))
        result[...] = jnp.concatenate(whole, 1).astype(BF16)

    with jax.named_scope("drain"):
        metas.wait_send()
        blocks.wait_send()
        sums.wait_send()
        for index in range(2):
            for way in range(2):
                row_blocks(way, index).wait_send()
        for stage in range(2):
            for part in range(2):
                chunks = hid.at[part, pl.ds(0, nx - 1)]
                one_way(chunks, chunks, sent_sem.at[stage, part], rs_sem.at[0, 0, 0, 0], x_dev(1)).wait_send()


def per_device(nx, ny, ng, tokens, cotangent, gates, expert_ids, capacity, w_gate, w_up, w_down):
    tok, width = tokens.shape
    top = expert_ids.shape[1]
    w, ff = w_gate.shape
    experts = capacity.shape[0]
    nl = nx * ny
    group = nl * tok
    slots = min(group * top // experts * 5 // 4, group)
    rows = ng * slots
    nj = w // LANES
    ns = 2 * nj
    fc = ff // nx
    part_rows = rows // 2
    top_rows = -(-part_rows // 32) * 16
    if top_rows >= part_rows:
        top_rows = part_rows // 2
    cap = capacity.reshape(1, experts)
    if experts < LANES:
        cap = jnp.pad(cap, ((0, 0), (0, LANES - experts)))
    vmem = pl.BlockSpec(memory_space=pltpu.VMEM)
    hbm = pl.BlockSpec(memory_space=pl.ANY)
    dma = pltpu.SemaphoreType.DMA
    both = pl.pallas_call(
        functools.partial(moe_kernel, nx, ny, ng, slots),
        out_shape=pltpu.VMEM((2 * tok, width), BF16),
        in_specs=[hbm] * 8,
        out_specs=vmem,
        scratch_shapes=[
            pltpu.VMEM((tok, width), BF16),
            pltpu.VMEM((tok, width), BF16),
            pltpu.VMEM((tok, top), BF16),
            pltpu.VMEM((tok, top), jnp.int32),
            pltpu.VMEM(cap.shape, jnp.int32),
            pltpu.VMEM((w, ff), BF16),
            pltpu.VMEM((w, ff), BF16),
            pltpu.VMEM((ff, w), BF16),
            pltpu.VMEM((8, LANES), F32),
            pltpu.VMEM((nl, 8, LANES), F32),
            pltpu.VMEM((nx, tok * ns, LANES), F32),
            pltpu.VMEM((nx, tok * ns, LANES), BF16),
            pltpu.VMEM((nl, tok * ns, LANES), BF16),
            pltpu.VMEM((nl * tok * ns, LANES), F32),
            pltpu.VMEM((group, rows), BF16),
            pltpu.VMEM((4, rows * nj, LANES), F32),
            pltpu.VMEM((2, ng, 2 * slots * nj, LANES), BF16),
            pltpu.VMEM((2, ng, 2 * slots * nj, LANES), BF16),
            pltpu.VMEM((2, rows, w), BF16),
            pltpu.VMEM((2, 2, 3, top_rows, fc), BF16),
            pltpu.VMEM((2, 2, 3, top_rows, fc), BF16),
        ] + [pltpu.VMEM((2, 2, 3, part_rows, fc), BF16)] * 6 + [
            pltpu.VMEM((5, 3, rows, fc), F32),
            pltpu.VMEM((2, nx, 3, part_rows, fc), BF16),
            pltpu.VMEM((2, rows, w), F32),
            pltpu.VMEM((nl * tok * ns, LANES), F32),
            pltpu.VMEM((nl, tok * ns, LANES), BF16),
            pltpu.VMEM((nl, tok * ns, LANES), BF16),
            dma((8,)),
            dma((2,)),
            dma((2,)),
            dma((2, 2, 2)),
            dma((4, 2, 2, 2)),
            dma((2, nx // 2, 2, 2)),
            dma((2, 2)),
            dma((2,)),
        ],
        compiler_params=pltpu.CompilerParams(
            collective_id=0, has_side_effects=True, vmem_limit_bytes=60 * 1024 * 1024),
    )(tokens, cotangent, gates, expert_ids, cap, w_gate, w_up, w_down)
    return both[:tok], both[tok:]


def solution(mesh):
    def run(tokens, cotangent, gates, expert_ids, capacity, w_gate, w_up, w_down):
        ng, local = mesh.shape["group"], mesh.shape["local"]
        w = w_gate.shape[0] // (ng * local)
        nx = tokens.shape[1] // w
        spec = P(("group", "local"), None)
        return jax.shard_map(
            functools.partial(per_device, nx, local // nx, ng),
            mesh=mesh,
            in_specs=(spec, spec, spec, spec, P(), spec, spec, P(None, ("group", "local"))),
            out_specs=(spec, spec),
            check_vma=False,
        )(tokens, cotangent, gates, expert_ids, capacity, w_gate, w_up, w_down)

    return run
```
